256 devices in a mesh: ctx: 64 (over z, y_lo, x), tp: 4 (over y_hi, core).
Axes of the slice: x: 4, y: 4 (y_hi: 2, y_lo: 2; y = y_hi * 2 + y_lo), z: 8, core: 2. Of those that a mesh axis runs over, the one named last changes fastest.
Arguments:
- queries: bfloat16 [8192, 6144], P('ctx', 'tp'), may hold values from -5 to 5
- keys_values: bfloat16 [8192, 2, 8, 128], P(('ctx', 'tp')), may hold values from -5 to 5
- segment_ids: int32 [8192], P('ctx'), may hold values from 0 to 3, never falling along the last dimension, each value on 1 to 6144 neighbouring positions
Outputs:
- attended: bfloat16 [8192, 6144], P('ctx', 'tp')
- log_sums: float32 [48, 8192], P('tp', 'ctx')
The draws below stay inside these ranges and needn't reach their ends.
Inputs may be any that keep to these rules, and one draw needn't show every extreme that they name: `segment_ids`: never falls along the tokens; every document has 1 to 6144 tokens, and one has exactly 6144.
All inputs are finite; a program needn't handle non-finite values.
Results may differ from the reference program's by a relative error of at most 0.0055.
Values may be sent and summed in bfloat16 or wider, within the bound.
A program may use at most 192 MiB of HBM per device.

```python
import math
import jax
import jax.numpy as jnp
import numpy as np
from jax import lax

Q_HEADS = 48
KV_HEADS = 8
HEAD = 128
DOCS = 4
TOKENS = 8192
DOC_MOST = 6144


def draw_queries(key, part):
    key = jax.random.fold_in(key, 11)
    first = jax.random.fold_in(key, 0)
    result = jnp.clip(jax.random.normal(first, (TOKENS, Q_HEADS, HEAD), jnp.float32), -5.0, 5.0)
    return result.reshape(TOKENS, Q_HEADS * HEAD).astype(jnp.bfloat16)


def draw_keys_values(key, part):
    key = jax.random.fold_in(key, 23)
    first = jax.random.fold_in(key, 0)
    third = jax.random.fold_in(key, 2)
    keys = jnp.clip(jax.random.normal(first, (TOKENS, KV_HEADS, HEAD), jnp.float32), -5.0, 5.0)
    values = jnp.clip(jax.random.normal(third, (TOKENS, KV_HEADS, HEAD), jnp.float32), -5.0, 5.0)
    return jnp.stack([keys, values], axis=1).astype(jnp.bfloat16)


def length_profile(count, total, limit, slope):
    loads = [(1 << 20) // math.isqrt(grade ** slope) + 1 for grade in range(2, count + 1)]
    rest, given = total - limit - (count - 1), [1] * (count - 1)
    while rest > 0:
        free = [i for i in range(count - 1) if given[i] < limit]
        whole, budget = sum([loads[i] for i in free]), rest
        for i in free:
            more = min(limit - given[i], max(1, budget * loads[i] // whole), rest)
            given[i] = given[i] + more
            rest = rest - more
    return np.array([limit] + given)


def uneven_parts(rng, amount, total, most, slope):
    if amount == 2:
        one = jax.random.randint(rng, (), max(1, total - most), min(most, total - 1) + 1)
        return jnp.stack([one, total - one])
    tallies = jnp.asarray(length_profile(amount, total, most, slope), jnp.int32)
    pairs = (amount - 1) // 2
    donor, receiver = tallies[1:1 + 2 * pairs:2], tallies[2:2 + 2 * pairs:2]
    margin = jnp.minimum(donor - 1, most - receiver)
    passed = jax.random.randint(jax.random.fold_in(rng, 1), (pairs,), 0, 1 << 20) % (margin + 1)
    tallies = tallies.at[1:1 + 2 * pairs:2].set(donor - passed).at[2:2 + 2 * pairs:2].set(receiver + passed)
    return tallies[jax.random.permutation(jax.random.fold_in(rng, 2), amount)]


def setup_inputs(seed: int = 0) -> dict:
    key_list = jax.random.split(jax.random.key(seed), 4)
    queries = draw_queries(jax.random.fold_in(key_list[3], 71), 0)
    keys_values = draw_keys_values(jax.random.fold_in(key_list[3], 71), 0)
    segment_ids = jnp.searchsorted(jnp.cumsum(uneven_parts(key_list[2], DOCS, TOKENS, DOC_MOST, 0)), jnp.arange(TOKENS), side="right").astype(jnp.int32)
    return dict(queries=queries, keys_values=keys_values, segment_ids=segment_ids)


def reference(queries, keys_values, segment_ids):
    group = Q_HEADS // KV_HEADS
    factor = HEAD ** -0.5
    rows = min(512, TOKENS)
    count = TOKENS // rows
    query_heads = queries.reshape(TOKENS, KV_HEADS, group, HEAD)
    key_pos = jnp.arange(TOKENS, dtype=jnp.int32)

    def one_tile(index):
        head = index // count
        start = (index % count) * rows
        query_block = lax.dynamic_slice_in_dim(query_heads, start, rows, 0)
        query_block = lax.dynamic_index_in_dim(query_block, head, 1, keepdims=False)
        keys = lax.dynamic_index_in_dim(keys_values[:, 0], head, 1, keepdims=False)
        values = lax.dynamic_index_in_dim(keys_values[:, 1], head, 1, keepdims=False)
        scores = jnp.einsum("qgd,kd->gqk", query_block.astype(jnp.float32), keys.astype(jnp.float32),
                            precision=lax.Precision.HIGHEST) * factor
        query_pos = start + jnp.arange(rows, dtype=jnp.int32)
        query_seg = lax.dynamic_slice_in_dim(segment_ids, start, rows, 0)
        allowed = (key_pos[None, :] <= query_pos[:, None]) & (segment_ids[None, :] == query_seg[:, None])
        scores = jnp.where(allowed[None], scores, jnp.float32(-1e30))
        rowmax = jnp.max(scores, axis=-1)
        weights = jnp.where(allowed[None], jnp.exp(scores - rowmax[..., None]), jnp.float32(0.0))
        total = jnp.sum(weights, axis=-1)
        rounded = weights.astype(jnp.bfloat16)
        output = jnp.einsum("gqk,kd->qgd", rounded.astype(jnp.float32), values.astype(jnp.float32),
                            precision=lax.Precision.HIGHEST)
        output = (output / jnp.transpose(total)[..., None]).astype(jnp.bfloat16)
        return output, rowmax + jnp.log(total)

    outputs, log_parts = lax.map(one_tile, jnp.arange(KV_HEADS * count, dtype=jnp.int32))
    outputs = outputs.reshape(KV_HEADS, count, rows, group, HEAD)
    attended = jnp.transpose(outputs, (1, 2, 0, 3, 4)).reshape(TOKENS, Q_HEADS * HEAD)
    log_parts = log_parts.reshape(KV_HEADS, count, group, rows)
    log_sums = jnp.transpose(log_parts, (0, 2, 1, 3)).reshape(Q_HEADS, TOKENS)
    return attended, log_sums
```

```python
import jax
import jax.numpy as jnp
from jax import lax
from jax.experimental import pallas as pl
from jax.experimental.pallas import tpu as pltpu
from jax.sharding import PartitionSpec as P

Q_HEADS = 48
KV_HEADS = 8
HEAD = 128
GROUP = Q_HEADS // KV_HEADS
WIDE = GROUP * HEAD
Z, YL, X, YH, CORES = 8, 2, 4, 2, 2
PIECE = 64
ROWS = GROUP * PIECE
KS = 272
PART = 528
FACTOR = HEAD ** (-0.5)
SLOPE = FACTOR * 1.4426950408889634
LOW = -1e30
MESH = pl.DeviceIdType.MESH


def kernel(
    q_ref, kvp_ref, out_ref, lse_ref,
    qbuf, stage, kv, qseg, acc, top, total, outbuf, lsend, lrecv,
    s1_send, s1_recv, q_send, q_recv, o_send, o_recv, l_send, l_recv,
    za_send, za_recv, zb_send, zb_recv, y_send, y_recv,
    sa_send, sa_recv, sb_send, sb_recv, sc_send, sc_recv,
):
    ctx = lax.axis_index("ctx")
    tp = lax.axis_index("tp")
    z, yl, x = ctx // 8, (ctx // 4) % 2, ctx % 4
    yh, c = tp // 2, tp % 2

    def dev(z_, yl_, x_, yh_, c_):
        return (z_ * 8 + yl_ * 4 + x_, yh_ * 2 + c_)

    z_up, z_down = (z + 1) % 8, (z + 7) % 8
    up_dev = dev(z_up, yl, x, yh, c)
    down_dev = dev(z_down, yl, x, yh, c)
    y_dev = dev(z, 1 - yl, x, yh, c)
    core_dev = dev(z, yl, x, yh, 1 - c)

    barrier = pltpu.get_barrier_semaphore()
    for dx in range(4):
        for dt in range(4):
            if dx or dt:
                to = (z * 8 + yl * 4 + (x + dx) % 4, (tp + dt) % 4)
                pl.semaphore_signal(barrier, inc=1, device_id=to, device_id_type=MESH)
    for to in (up_dev, down_dev, y_dev):
        pl.semaphore_signal(barrier, inc=1, device_id=to, device_id_type=MESH)
    pl.semaphore_wait(barrier, 18)

    def remote(src, dst, ssem, rsem, to):
        return pltpu.make_async_remote_copy(
            src_ref=src, dst_ref=dst, send_sem=ssem, recv_sem=rsem, device_id=to, device_id_type=MESH
        )

    def s1_copy(i):
        x2, yh2 = (x + i % 4) % 4, (yh + i // 4) % 2
        return remote(
            kvp_ref.at[yh2 * 4 + x2], stage.at[x * 2 + c], s1_send.at[i], s1_recv.at[x * 2 + c],
            dev(z, yl, x2, yh2, yh),
        )

    def s1_local():
        return pltpu.make_async_copy(kvp_ref.at[yh * 4 + x], stage.at[x * 2 + c], s1_recv.at[x * 2 + c])

    def q_parts(i):
        r, c2 = i // 2, (c + i % 2) % 2
        src = q_ref.at[
            pl.ds(pl.multiple_of(c2 * PIECE, PIECE), PIECE), r * WIDE:(r + 1) * WIDE
        ]
        return src, 2 * c + r, c2

    def q_copy(i):
        src, x2, c2 = q_parts(i)
        return remote(src, qbuf.at[x], q_send.at[i], q_recv.at[x], dev(z, yl, x2, yh, c2))

    def q_local(i):
        return pltpu.make_async_copy(q_parts(i)[0], qbuf.at[x], q_recv.at[x])

    def q_mine(i):
        return (2 * c + i // 2 == x) if i % 2 == 0 else (c != c)

    s1_mine = c == yh
    pl.when(s1_mine)(lambda: s1_local().start())
    pl.when(jnp.logical_not(s1_mine))(lambda: s1_copy(0).start())
    for i in range(1, 8):
        s1_copy(i).start()
    for i in range(4):
        if i % 2:
            q_copy(i).start()
        else:
            pl.when(q_mine(i))(lambda i=i: q_local(i).start())
            pl.when(jnp.logical_not(q_mine(i)))(lambda i=i: q_copy(i).start())

    acc[...] = jnp.zeros_like(acc)
    total[...] = jnp.zeros_like(total)
    top[...] = jnp.full_like(top, LOW)

    lane16 = lax.broadcasted_iota(jnp.int32, (16, 128), 1)
    row16 = lax.broadcasted_iota(jnp.int32, (16, 128), 0)
    lane64 = lax.broadcasted_iota(jnp.int32, (PIECE, 128), 1)
    row64 = lax.broadcasted_iota(jnp.int32, (PIECE, 128), 0)

    for i in range(8):
        pltpu.make_async_copy(stage.at[i], stage.at[i], s1_recv.at[i]).wait()
    mine = kv.at[z, yl, c]
    segs = []
    for x2 in range(4):
        for c2 in range(2):
            at = x2 * 64 + c2 * 32
            mine[at:at + 32, :] = stage[x2 * 2 + c2, 0:32, :]
            mine[KS + at:KS + at + 32, :] = stage[x2 * 2 + c2, 32:64, :]
        seg = stage[x2 * 2, 64:80, :].astype(jnp.float32)
        turned = pltpu.roll(seg, 64, axis=1)
        stay = c == x2 % 2
        segs.append(jnp.where(stay, seg, turned))
        column = jnp.sum(
            jnp.where(lane64 == row64 + c * 64, jnp.concatenate([seg] * 4, 0), 0.0), axis=1, keepdims=True
        )
        qseg[x2] = jnp.broadcast_to(column, (PIECE, 128))
    first = jnp.where(lane16 < 64, segs[0], segs[1])
    second = jnp.where(lane16 < 64, segs[2], segs[3])
    mine[256:KS, :] = jnp.where(row16 == 0, first, second).astype(jnp.bfloat16)

    def level(d, k):
        return z - k if d == 0 else (z + k) % 8

    def arrives(d, k):
        if d == 0:
            return z - k >= 0
        return (level(1, k) <= 2) & (k <= 3) & (k >= 1)

    def used(d, k):
        if d == 0:
            return z - k >= 0
        return arrives(1, k) & (level(1, k) < z)

    def leaves(d, k):
        if d == 0:
            return (z - k >= 0) & (z < 7) & (k <= 3)
        return (level(1, k) <= 2) & (k <= 2)

    def za(d, k):
        ref = kv.at[level(d, k), yl, c]
        return remote(ref, ref, za_send.at[d, k], za_recv.at[d, k + 1], (up_dev, down_dev)[d])

    def zb(d, k):
        ref = kv.at[level(d, k), 1 - yl, c, KS:PART]
        return remote(ref, ref, zb_send.at[d, k], zb_recv.at[d, k + 1], (up_dev, down_dev)[d])

    def yc(d, k, whole=False):
        ref = kv.at[level(d, k), yl, c] if whole else kv.at[level(d, k), yl, c, 0:KS]
        return remote(ref, ref, y_send.at[d, k], y_recv.at[d, k], y_dev)

    def sa(d, k):
        ref = kv.at[level(d, k), yl, c]
        return remote(ref, ref, sa_send.at[d, k], sa_recv.at[d, k], core_dev)

    def sb(d, k, whole=False):
        ref = kv.at[level(d, k), 1 - yl, c]
        if not whole:
            ref = ref.at[KS:PART]
        return remote(ref, ref, sb_send.at[d, k], sb_recv.at[d, k], core_dev)

    def sc(d, k):
        ref = kv.at[level(d, k), 1 - yl, c, 0:KS]
        return remote(ref, ref, sc_send.at[d, k], sc_recv.at[d, k], core_dev)

    def got(ref, sem):
        pltpu.make_async_copy(ref, ref, sem).wait()

    def pump_z(k):
        for d in range(2):
            @pl.when(arrives(d, k))
            def _():
                got(kv.at[level(d, k), yl, c], za_recv.at[d, k])
                pl.when(leaves(d, k))(lambda: za(d, k).start())
            @pl.when(used(d, k))
            def _():
                yc(d, k).start()
                sa(d, k).start()
        for d in range(2):
            @pl.when(arrives(d, k))
            def _():
                got(kv.at[level(d, k), 1 - yl, c, KS:PART], zb_recv.at[d, k])
                pl.when(leaves(d, k))(lambda: zb(d, k).start())
            @pl.when(used(d, k))
            def _():
                sb(d, k).start()

    def pump_y(k):
        for d in range(2):
            @pl.when(used(d, k))
            def _():
                got(kv.at[level(d, k), 1 - yl, c, 0:KS], y_recv.at[d, k])
                sc(d, k).start()

    def pump_core(k):
        for d in range(2):
            @pl.when(used(d, k))
            def _():
                got(kv.at[level(d, k), yl, 1 - c], sa_recv.at[d, k])
                got(kv.at[level(d, k), 1 - yl, 1 - c, KS:PART], sb_recv.at[d, k])
                got(kv.at[level(d, k), 1 - yl, 1 - c, 0:KS], sc_recv.at[d, k])

    yc(0, 0, True).start()
    sa(0, 0).start()
    for d in range(2):
        pl.when(leaves(d, 0))(lambda d=d: za(d, 0).start())
    got(kv.at[z, 1 - yl, c], y_recv.at[0, 0])
    for d in range(2):
        pl.when(leaves(d, 0))(lambda d=d: zb(d, 0).start())
    sb(0, 0, True).start()

    for i in range(4):
        got(qbuf.at[i], q_recv.at[i])
    got(kv.at[z, yl, 1 - c], sa_recv.at[0, 0])
    got(kv.at[z, 1 - yl, 1 - c], sb_recv.at[0, 0])

    blocks = [(a, b) for a in range(2) for b in range(2)]

    def scores(tile, lv):
        q = jnp.concatenate([qbuf[tile, :, g * HEAD:(g + 1) * HEAD] for g in range(GROUP)], 0)
        keys = jnp.concatenate([kv[lv, a, b, 0:256, :] for a, b in blocks], 0)
        return lax.dot_general(q, keys, (((1,), (1,)), ((), ())), preferred_element_type=jnp.float32)

    def bias(tile, lv, causal):
        own = qseg[tile]
        parts = []
        for a, b in blocks:
            rows = kv[lv, a, b, 256:KS, :].astype(jnp.float32)
            for half in range(2):
                same = own == rows[half:half + 1, :]
                if causal:
                    place = a * 512 + (half * 2 + lane64 // 64) * 128 + b * 64 + lane64 % 64
                    same = same & (place <= yl * 512 + tile * 128 + c * 64 + row64)
                parts.append(jnp.where(same, 0.0, LOW))
        return jnp.concatenate(parts, 1)

    def absorb(tile, lv, s, causal):
        s = s + jnp.concatenate([bias(tile, lv, causal)] * GROUP, 0)
        before = top[tile]
        now = jnp.maximum(before, jnp.max(s, axis=1, keepdims=True))
        top[tile] = now
        shrink = jnp.exp2((before - now) * SLOPE)
        weights = jnp.exp2((s - now[:, :1]) * SLOPE)
        total[tile] = total[tile] * shrink + jnp.sum(weights, axis=1, keepdims=True)
        values = jnp.concatenate([kv[lv, a, b, KS:PART, :] for a, b in blocks], 0)
        acc[tile] = acc[tile] * shrink + jnp.dot(
            weights.astype(jnp.bfloat16), values, preferred_element_type=jnp.float32
        )

    def compute(lv, causal=False):
        s = scores(0, lv)
        for tile in range(4):
            later = scores(tile + 1, lv) if tile < 3 else None
            absorb(tile, lv, s, causal)
            s = later

    compute(z, True)

    def step(k, carry):
        @pl.when((k >= 2) & used(0, k - 1))
        def _():
            compute(level(0, k - 1))

        pl.when(k <= 4)(lambda: pump_z(k))

        @pl.when(used(1, k - 1))
        def _():
            compute(level(1, k - 1))

        @pl.when(k <= 4)
        def _():
            pump_y(k)
            pump_core(k)

        return carry

    lax.fori_loop(1, 6, step, 0)

    r, home = x % 2, x // 2

    def o_copy(tile):
        dst = out_ref.at[
            pl.ds(pl.multiple_of(c * PIECE, PIECE), PIECE), pl.ds(pl.multiple_of(r * WIDE, WIDE), WIDE)
        ]
        return outbuf.at[tile], dst, o_send.at[tile], o_recv.at[r * 2 + c], dev(z, yl, tile, yh, home)

    def l_copy(tile):
        return (
            lsend.at[tile], lrecv.at[r * 2 + c], l_send.at[tile], l_recv.at[r * 2 + c],
            dev(z, yl, tile, yh, home),
        )

    for tile in range(4):
        sums = total[tile]
        done = (acc[tile] * (1.0 / sums)).astype(jnp.bfloat16)
        logs = top[tile] * FACTOR + jnp.log(sums)
        lines = jnp.zeros((16, 128), jnp.float32)
        for g in range(GROUP):
            outbuf[tile, :, g * HEAD:(g + 1) * HEAD] = done[g * PIECE:(g + 1) * PIECE, :]
            line = jnp.sum(
                jnp.where(lane64 == row64 + c * 64, logs[g * PIECE:(g + 1) * PIECE, :], 0.0),
                axis=0, keepdims=True,
            )
            lines = lines + jnp.where(row16 == r * GROUP + g, line, 0.0)
        lsend[tile] = lines
        here = (tile == x) & (home == c)

        @pl.when(here)
        def _():
            for src, dst, _, rsem, _ in (o_copy(tile), l_copy(tile)):
                pltpu.make_async_copy(src, dst, rsem).start()

        @pl.when(jnp.logical_not(here))
        def _():
            for copy in (o_copy(tile), l_copy(tile)):
                remote(*copy).start()

    pl.when(jnp.logical_not(s1_mine))(lambda: s1_copy(0).wait_send())
    for i in range(1, 8):
        s1_copy(i).wait_send()
    for i in range(4):
        if i % 2:
            q_copy(i).wait_send()
        else:
            pl.when(jnp.logical_not(q_mine(i)))(lambda i=i: q_copy(i).wait_send())
    yc(0, 0, True).wait_send()
    sa(0, 0).wait_send()
    sb(0, 0, True).wait_send()
    for d in range(2):
        @pl.when(leaves(d, 0))
        def _():
            za(d, 0).wait_send()
            zb(d, 0).wait_send()

    def drain(k, carry):
        for d in range(2):
            @pl.when(arrives(d, k) & leaves(d, k))
            def _():
                za(d, k).wait_send()
                zb(d, k).wait_send()
            @pl.when(used(d, k))
            def _():
                yc(d, k).wait_send()
                sa(d, k).wait_send()
                sb(d, k).wait_send()
                sc(d, k).wait_send()
        return carry

    lax.fori_loop(1, 5, drain, 0)
    for tile in range(4):
        @pl.when(jnp.logical_not((tile == x) & (home == c)))
        def _():
            remote(*o_copy(tile)).wait_send()
            remote(*l_copy(tile)).wait_send()
    for i in range(4):
        got(lrecv.at[i], l_recv.at[i])
    lse_ref[...] = (lrecv[0] + lrecv[1] + lrecv[2] + lrecv[3])[:2 * GROUP, :]
    for i in range(4):
        got(outbuf.at[i], o_recv.at[i])


def shards(queries, keys_values, segment_ids):
    pieces = jnp.transpose(keys_values, (2, 1, 0, 3)).reshape(KV_HEADS, 64, HEAD)
    marks = jnp.broadcast_to(segment_ids.astype(jnp.bfloat16)[None, None, :], (KV_HEADS, 16, 128))
    kvp = jnp.concatenate([pieces, marks], axis=1)
    dma = pltpu.SemaphoreType.DMA
    bf, f32 = jnp.bfloat16, jnp.float32
    return pl.pallas_call(
        kernel,
        out_shape=(
            jax.ShapeDtypeStruct((128, 2 * WIDE), bf),
            jax.ShapeDtypeStruct((2 * GROUP, 128), f32),
        ),
        in_specs=[pl.BlockSpec(memory_space=pl.ANY)] * 2,
        out_specs=(pl.BlockSpec(memory_space=pl.ANY), pl.BlockSpec(memory_space=pltpu.VMEM)),
        scratch_shapes=[
            pltpu.VMEM((4, PIECE, WIDE), bf),
            pltpu.VMEM((8, 80, 128), bf),
            pltpu.VMEM((Z, YL, CORES, PART, HEAD), bf),
            pltpu.VMEM((4, PIECE, 128), f32),
            pltpu.VMEM((4, ROWS, HEAD), f32),
            pltpu.VMEM((4, ROWS, 128), f32),
            pltpu.VMEM((4, ROWS, 128), f32),
            pltpu.VMEM((4, PIECE, WIDE), bf),
            pltpu.VMEM((4, 16, 128), f32),
            pltpu.VMEM((4, 16, 128), f32),
            dma((8,)), dma((8,)), dma((4,)), dma((4,)), dma((4,)), dma((4,)), dma((4,)), dma((4,)),
        ] + [dma((2, 5))] * 12,
        compiler_params=pltpu.CompilerParams(
            collective_id=0, has_side_effects=True, vmem_limit_bytes=48 * 2**20
        ),
        cost_estimate=pl.CostEstimate(flops=6 * 10**9, bytes_accessed=10**6, transcendentals=12 * 10**6),
    )(queries, kvp)


def solution(mesh):
    placed = (P("ctx", "tp"), P(("ctx", "tp"), None, None, None), P("ctx"))
    return jax.shard_map(
        shards,
        mesh=mesh,
        in_specs=placed,
        out_specs=(P("ctx", "tp"), P("tp", "ctx")),
        check_vma=False,
    )
```

```python
import jax
import jax.numpy as jnp
from jax import lax
from jax.experimental import pallas as pl
from jax.experimental.pallas import tpu as pltpu
from jax.sharding import PartitionSpec as P

Q_HEADS = 48
KV_HEADS = 8
HEAD = 128
GROUP = Q_HEADS // KV_HEADS
WIDE = GROUP * HEAD
Z, YL, X, YH, CORES = 8, 2, 4, 2, 2
PIECE = 64
HALF = 32
ROWS = GROUP * HALF
TILES = 8
KS = 272
PART = 528
FACTOR = HEAD ** (-0.5)
SLOPE = FACTOR * 1.4426950408889634
LOW = -1e30
MESH = pl.DeviceIdType.MESH


def kernel(
    q_ref, kvp_ref, out_ref, lse_ref,
    qbuf, stage, kv, qseg, acc, top, total, outbuf, lsend, lrecv,
    s1_send, s1_recv, q_send, q_recv, o_send, o_recv, l_send, l_recv,
    za_send, za_recv, zb_send, zb_recv, y_send, y_recv,
    sa_send, sa_recv, sb_send, sb_recv, sc_send, sc_recv,
):
    ctx = lax.axis_index("ctx")
    tp = lax.axis_index("tp")
    z, yl, x = ctx // 8, (ctx // 4) % 2, ctx % 4
    yh, c = tp // 2, tp % 2

    def dev(z_, yl_, x_, yh_, c_):
        return (z_ * 8 + yl_ * 4 + x_, yh_ * 2 + c_)

    z_up, z_down = (z + 1) % 8, (z + 7) % 8
    up_dev = dev(z_up, yl, x, yh, c)
    down_dev = dev(z_down, yl, x, yh, c)
    y_dev = dev(z, 1 - yl, x, yh, c)
    core_dev = dev(z, yl, x, yh, 1 - c)

    barrier = pltpu.get_barrier_semaphore()
    for dx in range(4):
        for dt in range(4):
            if dx or dt:
                to = (z * 8 + yl * 4 + (x + dx) % 4, (tp + dt) % 4)
                pl.semaphore_signal(barrier, inc=1, device_id=to, device_id_type=MESH)
    for to in (up_dev, down_dev, y_dev):
        pl.semaphore_signal(barrier, inc=1, device_id=to, device_id_type=MESH)
    pl.semaphore_wait(barrier, 18)

    def remote(src, dst, ssem, rsem, to):
        return pltpu.make_async_remote_copy(
            src_ref=src, dst_ref=dst, send_sem=ssem, recv_sem=rsem, device_id=to, device_id_type=MESH
        )

    def s1_copy(i):
        x2, yh2 = (x + i % 4) % 4, (yh + i // 4) % 2
        return remote(
            kvp_ref.at[yh2 * 4 + x2], stage.at[x * 2 + c], s1_send.at[i], s1_recv.at[x * 2 + c],
            dev(z, yl, x2, yh2, yh),
        )

    def s1_local():
        return pltpu.make_async_copy(kvp_ref.at[yh * 4 + x], stage.at[x * 2 + c], s1_recv.at[x * 2 + c])

    def q_parts(i):
        r, c2 = i // 2, (c + i % 2) % 2
        src = q_ref.at[
            pl.ds(pl.multiple_of(c2 * PIECE, PIECE), PIECE), r * WIDE:(r + 1) * WIDE
        ]
        return src, 2 * c + r, c2

    def q_copy(i):
        src, x2, c2 = q_parts(i)
        return remote(src, qbuf.at[x], q_send.at[i], q_recv.at[x], dev(z, yl, x2, yh, c2))

    def q_local(i):
        return pltpu.make_async_copy(q_parts(i)[0], qbuf.at[x], q_recv.at[x])

    def q_mine(i):
        return (2 * c + i // 2 == x) if i % 2 == 0 else (c != c)

    s1_mine = c == yh
    pl.when(s1_mine)(lambda: s1_local().start())
    pl.when(jnp.logical_not(s1_mine))(lambda: s1_copy(0).start())
    for i in range(1, 8):
        s1_copy(i).start()
    for i in range(4):
        if i % 2:
            q_copy(i).start()
        else:
            pl.when(q_mine(i))(lambda i=i: q_local(i).start())
            pl.when(jnp.logical_not(q_mine(i)))(lambda i=i: q_copy(i).start())

    acc[...] = jnp.zeros_like(acc)
    total[...] = jnp.zeros_like(total)
    top[...] = jnp.full_like(top, LOW)

    lane16 = lax.broadcasted_iota(jnp.int32, (16, 128), 1)
    row16 = lax.broadcasted_iota(jnp.int32, (16, 128), 0)
    lane64 = lax.broadcasted_iota(jnp.int32, (PIECE, 128), 1)
    row64 = lax.broadcasted_iota(jnp.int32, (PIECE, 128), 0)
    lane32 = lax.broadcasted_iota(jnp.int32, (HALF, 128), 1)
    row32 = lax.broadcasted_iota(jnp.int32, (HALF, 128), 0)

    for i in range(8):
        pltpu.make_async_copy(stage.at[i], stage.at[i], s1_recv.at[i]).wait()
    mine = kv.at[z, yl, c]
    segs = []
    for x2 in range(4):
        for c2 in range(2):
            at = x2 * 64 + c2 * 32
            mine[at:at + 32, :] = stage[x2 * 2 + c2, 0:32, :]
            mine[KS + at:KS + at + 32, :] = stage[x2 * 2 + c2, 32:64, :]
        seg = stage[x2 * 2, 64:80, :].astype(jnp.float32)
        turned = pltpu.roll(seg, 64, axis=1)
        stay = c == x2 % 2
        segs.append(jnp.where(stay, seg, turned))
        column = jnp.sum(
            jnp.where(lane64 == row64 + c * 64, jnp.concatenate([seg] * 4, 0), 0.0), axis=1, keepdims=True
        )
        qseg[x2] = jnp.broadcast_to(column, (PIECE, 128))
    first = jnp.where(lane16 < 64, segs[0], segs[1])
    second = jnp.where(lane16 < 64, segs[2], segs[3])
    mine[256:KS, :] = jnp.where(row16 == 0, first, second).astype(jnp.bfloat16)

    def level(d, k):
        return z - k if d == 0 else (z + k) % 8

    def arrives(d, k):
        if d == 0:
            return z - k >= 0
        return (level(1, k) <= 2) & (k <= 3) & (k >= 1)

    def used(d, k):
        if d == 0:
            return z - k >= 0
        return arrives(1, k) & (level(1, k) < z)

    def leaves(d, k):
        if d == 0:
            return (z - k >= 0) & (z < 7) & (k <= 3)
        return (level(1, k) <= 2) & (k <= 2)

    def za(d, k):
        ref = kv.at[level(d, k), yl, c]
        return remote(ref, ref, za_send.at[d], za_recv.at[d, k], (up_dev, down_dev)[d])

    def zb(d, k):
        ref = kv.at[level(d, k), 1 - yl, c, KS:PART]
        return remote(ref, ref, zb_send.at[d], zb_recv.at[d, k], (up_dev, down_dev)[d])

    def yc(d, k, whole=False):
        ref = kv.at[level(d, k), yl, c] if whole else kv.at[level(d, k), yl, c, 0:KS]
        return remote(ref, ref, y_send.at[d], y_recv.at[d, k], y_dev)

    def sa(d, k):
        ref = kv.at[level(d, k), yl, c]
        return remote(ref, ref, sa_send.at[d], sa_recv.at[d, k], core_dev)

    def sb(d, k, whole=False):
        ref = kv.at[level(d, k), 1 - yl, c]
        if not whole:
            ref = ref.at[KS:PART]
        return remote(ref, ref, sb_send.at[d], sb_recv.at[d, k], core_dev)

    def sc(d, k):
        ref = kv.at[level(d, k), 1 - yl, c, 0:KS]
        return remote(ref, ref, sc_send.at[d], sc_recv.at[d, k], core_dev)

    def got(ref, sem):
        pltpu.make_async_copy(ref, ref, sem).wait()

    def pump_a(k):
        for d in range(2):
            @pl.when(leaves(d, k - 1))
            def _():
                za(d, k - 1).wait_send()

            @pl.when(arrives(d, k))
            def _():
                got(kv.at[level(d, k), yl, c], za_recv.at[d, k - 1])
                pl.when(leaves(d, k))(lambda: za(d, k).start())

            if isinstance(k, int):
                if d == 0:
                    yc(0, 0, True).wait_send()
                    sa(0, 0).wait_send()
            else:
                @pl.when(used(d, k - 1))
                def _():
                    yc(d, k - 1).wait_send()
                    sa(d, k - 1).wait_send()

            @pl.when(used(d, k))
            def _():
                yc(d, k).start()
                sa(d, k).start()

    def pump_b(k):
        for d in range(2):
            @pl.when(leaves(d, k - 1))
            def _():
                zb(d, k - 1).wait_send()

            @pl.when(arrives(d, k))
            def _():
                got(kv.at[level(d, k), 1 - yl, c, KS:PART], zb_recv.at[d, k - 1])
                pl.when(leaves(d, k))(lambda: zb(d, k).start())

            if d == 0:
                @pl.when(k == 1)
                def _():
                    sb(0, 0, True).wait_send()

            @pl.when(used(d, k - 1) & (k >= 2))
            def _():
                sb(d, k - 1).wait_send()

            @pl.when(used(d, k))
            def _():
                sb(d, k).start()

    def pump_y(k):
        for d in range(2):
            @pl.when(used(d, k - 1) & (k >= 2))
            def _():
                sc(d, k - 1).wait_send()

            @pl.when(used(d, k))
            def _():
                got(kv.at[level(d, k), 1 - yl, c, 0:KS], y_recv.at[d, k])
                sc(d, k).start()

    def await_a(k):
        for d in range(2):
            @pl.when(used(d, k))
            def _():
                got(kv.at[level(d, k), yl, 1 - c], sa_recv.at[d, k])

    def await_b(k):
        for d in range(2):
            @pl.when(used(d, k))
            def _():
                got(kv.at[level(d, k), 1 - yl, 1 - c, KS:PART], sb_recv.at[d, k])
                got(kv.at[level(d, k), 1 - yl, 1 - c, 0:KS], sc_recv.at[d, k])

    yc(0, 0, True).start()
    for d in range(2):
        pl.when(leaves(d, 0))(lambda d=d: za(d, 0).start())
    sa(0, 0).start()
    got(kv.at[z, 1 - yl, c], y_recv.at[0, 0])
    for d in range(2):
        pl.when(leaves(d, 0))(lambda d=d: zb(d, 0).start())
    sb(0, 0, True).start()
    pump_a(1)
    for i in range(4):
        got(qbuf.at[i], q_recv.at[i])
    got(kv.at[z, yl, 1 - c], sa_recv.at[0, 0])
    got(kv.at[z, 1 - yl, 1 - c], sb_recv.at[0, 0])

    def lanes(unit):
        return [(lv, y, b) for lv, y in unit for b in range(2)]

    def scores(tile, unit):
        xt, h = tile
        q = jnp.concatenate(
            [qbuf[xt, h * HALF:(h + 1) * HALF, g * HEAD:(g + 1) * HEAD] for g in range(GROUP)], 0
        )
        keys = jnp.concatenate([kv[lv, y, b, 0:256, :] for lv, y, b in lanes(unit)], 0)
        return lax.dot_general(q, keys, (((1,), (1,)), ((), ())), preferred_element_type=jnp.float32)

    def bias(tile, unit, causal):
        xt, h = tile
        own = qseg[xt, h * HALF:(h + 1) * HALF, :]
        parts = []
        for lv, y, b in lanes(unit):
            rows = kv[lv, y, b, 256:KS, :].astype(jnp.float32)
            for half in range(2):
                same = own == rows[half:half + 1, :]
                if causal:
                    place = y * 512 + (half * 2 + lane32 // 64) * 128 + b * 64 + lane32 % 64
                    same = same & (place <= yl * 512 + xt * 128 + c * 64 + h * HALF + row32)
                parts.append(jnp.where(same, 0.0, LOW))
        return jnp.concatenate(parts, 1)

    def absorb(tile, unit, s, causal):
        at = tile[0] * 2 + tile[1]
        s = s + jnp.concatenate([bias(tile, unit, causal)] * GROUP, 0)
        before = top[at]
        now = jnp.maximum(before, jnp.max(s, axis=1, keepdims=True))
        top[at] = now
        shrink = jnp.exp2((before - now) * SLOPE)
        weights = jnp.exp2((s - now[:, :1]) * SLOPE)
        values = jnp.concatenate([kv[lv, y, b, KS:PART, :] for lv, y, b in lanes(unit)], 0)
        values = jnp.concatenate([values, jnp.ones_like(values)], 1)
        sums = jnp.dot(weights.astype(jnp.bfloat16), values, preferred_element_type=jnp.float32)
        acc[at] = acc[at] * shrink + sums[:, :HEAD]
        total[at] = total[at] * shrink + sums[:, HEAD:]

    TILED = [(xt, h) for xt in range(4) for h in range(2)]

    def compute(unit, tiles=TILED, causal=False, after=None):
        s = scores(tiles[0], unit)
        for i, tile in enumerate(tiles):
            later = scores(tiles[i + 1], unit) if i + 1 < len(tiles) else None
            absorb(tile, unit, s, causal)
            if after is not None and i % 2:
                after(i // 2)
            s = later

    def both(k):
        return used(0, k) & used(1, k)

    def unit_a(k):
        return [(level(0, k), yl), (level(1, k), yl)]

    def unit_b(k):
        two = both(k)
        return [
            (level(0, k), jnp.where(two, 1 - yl, yl)),
            (jnp.where(two, level(1, k), level(0, k)), 1 - yl),
        ]

    compute([(z, 0), (z, 1)], causal=True)

    def step(k, carry):
        @pl.when((k >= 2) & used(0, k - 1))
        def _():
            compute(unit_b(k - 1))

        pump_b(k)
        await_a(k)
        pl.when(both(k))(lambda: compute(unit_a(k), TILED[:4]))
        pump_y(k)
        pl.when(both(k))(lambda: compute(unit_a(k), TILED[4:]))
        pl.when(k <= 3)(lambda: pump_a(k + 1))
        await_b(k)
        return carry

    lax.fori_loop(1, 5, step, 0)

    r, home = x % 2, x // 2

    def block(i):
        return (x + 1 + i) % 4

    def o_copy(i):
        dst = out_ref.at[
            pl.ds(pl.multiple_of(c * PIECE, PIECE), PIECE), pl.ds(pl.multiple_of(r * WIDE, WIDE), WIDE)
        ]
        xt = block(i)
        return outbuf.at[xt], dst, o_send.at[i], o_recv.at[r * 2 + c], dev(z, yl, xt, yh, home)

    def l_copy(i):
        xt = block(i)
        return lsend.at[xt], lrecv.at[r * 2 + c], l_send.at[i], l_recv.at[r * 2 + c], dev(z, yl, xt, yh, home)

    def finish(i):
        xt = block(i)
        lines = jnp.zeros((16, 128), jnp.float32)
        for h in range(2):
            sums = total[xt * 2 + h]
            done = (acc[xt * 2 + h] * (1.0 / sums)).astype(jnp.bfloat16)
            logs = top[xt * 2 + h] * FACTOR + jnp.log(sums)
            for g in range(GROUP):
                rows = slice(g * HALF, (g + 1) * HALF)
                outbuf[xt, h * HALF:(h + 1) * HALF, g * HEAD:(g + 1) * HEAD] = done[rows, :]
                line = jnp.sum(
                    jnp.where(lane32 == row32 + c * 64 + h * HALF, logs[rows, :], 0.0),
                    axis=0, keepdims=True,
                )
                lines = lines + jnp.where(row16 == r * GROUP + g, line, 0.0)
        lsend[xt] = lines
        if i < 3:
            remote(*o_copy(i)).start()
            remote(*l_copy(i)).start()
        else:
            @pl.when(home == c)
            def _():
                for src, dst, _, rsem, _ in (o_copy(i), l_copy(i)):
                    pltpu.make_async_copy(src, dst, rsem).start()

            @pl.when(home != c)
            def _():
                remote(*o_copy(i)).start()
                remote(*l_copy(i)).start()

    @pl.when(used(0, 4))
    def _():
        tiles = [(block(i), h) for i in range(4) for h in range(2)]
        compute([(level(0, 4), 0), (level(0, 4), 1)], tiles, after=finish)

    @pl.when(jnp.logical_not(used(0, 4)))
    def _():
        for i in range(4):
            finish(i)

    pl.when(jnp.logical_not(s1_mine))(lambda: s1_copy(0).wait_send())
    for i in range(1, 8):
        s1_copy(i).wait_send()
    for i in range(4):
        if i % 2:
            q_copy(i).wait_send()
        else:
            pl.when(jnp.logical_not(q_mine(i)))(lambda i=i: q_copy(i).wait_send())

    @pl.when(used(0, 4))
    def _():
        yc(0, 4).wait_send()
        sa(0, 4).wait_send()
        sb(0, 4).wait_send()
        sc(0, 4).wait_send()

    for i in range(3):
        remote(*o_copy(i)).wait_send()
        remote(*l_copy(i)).wait_send()

    @pl.when(home != c)
    def _():
        remote(*o_copy(3)).wait_send()
        remote(*l_copy(3)).wait_send()

    for i in range(4):
        got(lrecv.at[i], l_recv.at[i])
    lse_ref[...] = (lrecv[0] + lrecv[1] + lrecv[2] + lrecv[3])[:2 * GROUP, :]
    for i in range(4):
        got(outbuf.at[i], o_recv.at[i])


def shards(queries, keys_values, segment_ids):
    pieces = jnp.transpose(keys_values, (2, 1, 0, 3)).reshape(KV_HEADS, 64, HEAD)
    marks = jnp.broadcast_to(segment_ids.astype(jnp.bfloat16)[None, None, :], (KV_HEADS, 16, 128))
    kvp = jnp.concatenate([pieces, marks], axis=1)
    dma = pltpu.SemaphoreType.DMA
    bf, f32 = jnp.bfloat16, jnp.float32
    return pl.pallas_call(
        kernel,
        out_shape=(
            jax.ShapeDtypeStruct((128, 2 * WIDE), bf),
            jax.ShapeDtypeStruct((2 * GROUP, 128), f32),
        ),
        in_specs=[pl.BlockSpec(memory_space=pl.ANY)] * 2,
        out_specs=(pl.BlockSpec(memory_space=pl.ANY), pl.BlockSpec(memory_space=pltpu.VMEM)),
        scratch_shapes=[
            pltpu.VMEM((4, PIECE, WIDE), bf),
            pltpu.VMEM((8, 80, 128), bf),
            pltpu.VMEM((Z, YL, CORES, PART, HEAD), bf),
            pltpu.VMEM((4, PIECE, 128), f32),
            pltpu.VMEM((TILES, ROWS, HEAD), f32),
            pltpu.VMEM((TILES, ROWS, 128), f32),
            pltpu.VMEM((TILES, ROWS, 128), f32),
            pltpu.VMEM((4, PIECE, WIDE), bf),
            pltpu.VMEM((4, 16, 128), f32),
            pltpu.VMEM((4, 16, 128), f32),
            dma((8,)), dma((8,)), dma((4,)), dma((4,)), dma((4,)), dma((4,)), dma((4,)), dma((4,)),
        ] + [dma((2,)), dma((2, 4))] * 2 + [dma((2,)), dma((2, 5))] * 4,
        compiler_params=pltpu.CompilerParams(
            collective_id=0, has_side_effects=True, vmem_limit_bytes=48 * 2**20
        ),
        cost_estimate=pl.CostEstimate(flops=6 * 10**9, bytes_accessed=10**6, transcendentals=12 * 10**6),
    )(queries, kvp)


def solution(mesh):
    placed = (P("ctx", "tp"), P(("ctx", "tp"), None, None, None), P("ctx"))
    return jax.shard_map(
        shards,
        mesh=mesh,
        in_specs=placed,
        out_specs=(P("ctx", "tp"), P("tp", "ctx")),
        check_vma=False,
    )
```

```python
import jax
import jax.numpy as jnp
from jax import lax
from jax.experimental import pallas as pl
from jax.experimental.pallas import tpu as pltpu
from jax.sharding import PartitionSpec as P

Q_HEADS = 48
KV_HEADS = 8
HEAD = 128
GROUP = Q_HEADS // KV_HEADS
WIDE = GROUP * HEAD
Z, YL, X, YH, CORES = 8, 2, 4, 2, 2
PIECE = 64
HALF = 32
ROWS = GROUP * HALF
TILES = 8
KS = 272
PART = 528
CUT = 352
FACTOR = HEAD ** (-0.5)
SLOPE = FACTOR * 1.4426950408889634
LOW = -1e30
MESH = pl.DeviceIdType.MESH


def kernel(
    q_ref, pieces, out_ref, lse_ref,
    qbuf, stage, kv, qseg, acc, top, total, outbuf, lsend, lrecv,
    s1_send, s1_recv, q_send, q_recv, o_send, o_recv, l_send, l_recv,
    za_send, za_recv, zb_send, zb_recv, y_send, y_recv, yb_send, yb_recv,
    sa_send, sa_recv, sb_send, sb_recv, sc_send, sc_recv,
):
    ctx = lax.axis_index("ctx")
    tp = lax.axis_index("tp")
    z, yl, x = ctx // 8, (ctx // 4) % 2, ctx % 4
    yh, c = tp // 2, tp % 2

    def dev(z_, yl_, x_, yh_, c_):
        return (z_ * 8 + yl_ * 4 + x_, yh_ * 2 + c_)

    z_up, z_down = (z + 1) % 8, (z + 7) % 8
    up_dev = dev(z_up, yl, x, yh, c)
    down_dev = dev(z_down, yl, x, yh, c)
    y_dev = dev(z, 1 - yl, x, yh, c)
    core_dev = dev(z, yl, x, yh, 1 - c)

    barrier = pltpu.get_barrier_semaphore()
    for dx in range(4):
        for dt in range(4):
            if dx or dt:
                to = (z * 8 + yl * 4 + (x + dx) % 4, (tp + dt) % 4)
                pl.semaphore_signal(barrier, inc=1, device_id=to, device_id_type=MESH)
    for to in (up_dev, down_dev, y_dev):
        pl.semaphore_signal(barrier, inc=1, device_id=to, device_id_type=MESH)

    acc[...] = jnp.zeros_like(acc)
    total[...] = jnp.zeros_like(total)
    top[...] = jnp.full_like(top, LOW)
    pl.semaphore_wait(barrier, 18)

    def remote(src, dst, ssem, rsem, to):
        return pltpu.make_async_remote_copy(
            src_ref=src, dst_ref=dst, send_sem=ssem, recv_sem=rsem, device_id=to, device_id_type=MESH
        )

    def s1_copy(i):
        x2, yh2 = (x + i % 4) % 4, (yh + i // 4) % 2
        return remote(
            pieces.at[yh2 * 4 + x2], stage.at[x * 2 + c], s1_send, s1_recv,
            dev(z, yl, x2, yh2, yh),
        )

    def s1_local():
        return pltpu.make_async_copy(pieces.at[yh * 4 + x], stage.at[x * 2 + c], s1_recv)

    def q_parts(i):
        r, c2 = i // 2, (c + i % 2) % 2
        src = q_ref.at[
            pl.ds(pl.multiple_of(c2 * PIECE, PIECE), PIECE), r * WIDE:(r + 1) * WIDE
        ]
        return src, 2 * c + r, c2

    def q_copy(i):
        src, x2, c2 = q_parts(i)
        return remote(src, qbuf.at[x], q_send, q_recv, dev(z, yl, x2, yh, c2))

    def q_local(i):
        return pltpu.make_async_copy(q_parts(i)[0], qbuf.at[x], q_recv)

    def q_mine(i):
        return (2 * c + i // 2 == x) if i % 2 == 0 else (c != c)

    s1_mine = c == yh
    pl.when(s1_mine)(lambda: s1_local().start())
    pl.when(jnp.logical_not(s1_mine))(lambda: s1_copy(0).start())
    for i in range(1, 8):
        s1_copy(i).start()
    lane16 = lax.broadcasted_iota(jnp.int32, (16, 128), 1)
    row16 = lax.broadcasted_iota(jnp.int32, (16, 128), 0)
    lane64 = lax.broadcasted_iota(jnp.int32, (PIECE, 128), 1)
    row64 = lax.broadcasted_iota(jnp.int32, (PIECE, 128), 0)
    lane32 = lax.broadcasted_iota(jnp.int32, (HALF, 128), 1)
    row32 = lax.broadcasted_iota(jnp.int32, (HALF, 128), 0)

    pltpu.make_async_copy(stage, stage, s1_recv).wait()
    mine = kv.at[z, yl, c]
    segs = []
    for x2 in range(4):
        for c2 in range(2):
            at = x2 * 64 + c2 * 32
            mine[at:at + 32, :] = stage[x2 * 2 + c2, 0:32, :]
            mine[KS + at:KS + at + 32, :] = stage[x2 * 2 + c2, 32:64, :]
        seg = stage[x2 * 2, 64:80, :].astype(jnp.float32)
        segs.append(jnp.where(c == x2 % 2, seg, pltpu.roll(seg, 64, axis=1)))
    first = jnp.where(lane16 < 64, segs[0], segs[1])
    second = jnp.where(lane16 < 64, segs[2], segs[3])
    mine[256:KS, :] = jnp.where(row16 == 0, first, second).astype(jnp.bfloat16)

    def level(d, k):
        return z - k if d == 0 else (z + k) % 8

    def arrives(d, k):
        if d == 0:
            return z - k >= 0
        return (level(1, k) <= 2) & (k <= 3) & (k >= 1)

    def used(d, k):
        if d == 0:
            return z - k >= 0
        return arrives(1, k) & (level(1, k) < z)

    def leaves(d, k):
        if d == 0:
            return (z - k >= 0) & (z < 7) & (k <= 3)
        return (level(1, k) <= 2) & (k <= 2)

    def za(d, k):
        ref = kv.at[level(d, k), yl, c, 0:CUT]
        return remote(ref, ref, za_send.at[d], za_recv.at[d, k], (up_dev, down_dev)[d])

    def zb(d, k, y):
        ref = kv.at[level(d, k), y, c, CUT:PART]
        return remote(ref, ref, zb_send.at[d], zb_recv.at[d, k], (up_dev, down_dev)[d])

    def yc(d, k):
        ref = kv.at[level(d, k), yl, c, 0:CUT]
        return remote(ref, ref, y_send.at[d], y_recv.at[d, k], y_dev)

    def y_rest():
        ref = kv.at[z, yl, c, CUT:PART]
        return remote(ref, ref, yb_send, yb_recv, y_dev)

    def sa(d, k):
        ref = kv.at[level(d, k), yl, c, 0:CUT]
        return remote(ref, ref, sa_send.at[d], sa_recv.at[d, k], core_dev)

    def sb(d, k, y):
        ref = kv.at[level(d, k), y, c, CUT:PART]
        return remote(ref, ref, sb_send.at[d], sb_recv.at[d, k], core_dev)

    def sc(d, k):
        ref = kv.at[level(d, k), 1 - yl, c, 0:CUT]
        return remote(ref, ref, sc_send.at[d], sc_recv.at[d, k], core_dev)

    def got(ref, sem):
        pltpu.make_async_copy(ref, ref, sem).wait()

    def got_two(sem):
        got(kv.at[0, 0, 0, 0:2 * (PART - CUT)], sem)

    def pump_a(k):
        for d in range(2):
            @pl.when(leaves(d, k - 1))
            def _():
                za(d, k - 1).wait_send()

            @pl.when(arrives(d, k))
            def _():
                got(kv.at[level(d, k), yl, c, 0:CUT], za_recv.at[d, k - 1])
                pl.when(leaves(d, k))(lambda: za(d, k).start())

            @pl.when(used(d, k - 1))
            def _():
                yc(d, k - 1).wait_send()
                sa(d, k - 1).wait_send()

            @pl.when(used(d, k))
            def _():
                yc(d, k).start()
                sa(d, k).start()

    def pump_b(k):
        for d in range(2):
            @pl.when(leaves(d, k - 1))
            def _():
                got_two(zb_send.at[d])

            @pl.when(arrives(d, k))
            def _():
                got_two(zb_recv.at[d, k - 1])

                @pl.when(leaves(d, k))
                def _():
                    zb(d, k, yl).start()
                    zb(d, k, 1 - yl).start()

            pl.when(used(d, k - 1))(lambda: got_two(sb_send.at[d]))

            @pl.when(used(d, k))
            def _():
                sb(d, k, yl).start()
                sb(d, k, 1 - yl).start()

    def pump_y(k):
        for d in range(2):
            pl.when(used(d, k - 1) & (k >= 1))(lambda: sc(d, k - 1).wait_send())

            @pl.when(used(d, k))
            def _():
                got(kv.at[level(d, k), 1 - yl, c, 0:CUT], y_recv.at[d, k])
                sc(d, k).start()

    def await_a(k):
        for d in range(2):
            @pl.when(used(d, k))
            def _():
                got(kv.at[level(d, k), yl, 1 - c, 0:CUT], sa_recv.at[d, k])
                got_two(sb_recv.at[d, k])

    def await_b(k):
        for d in range(2):
            @pl.when(used(d, k))
            def _():
                got(kv.at[level(d, k), 1 - yl, 1 - c, 0:CUT], sc_recv.at[d, k])

    for d in range(2):
        pl.when(leaves(d, 0))(lambda d=d: za(d, 0).start())
    y_rest().start()
    for d in range(2):
        pl.when(leaves(d, 0))(lambda d=d: zb(d, 0, yl).start())
    yc(0, 0).start()
    sa(0, 0).start()
    sb(0, 0, yl).start()
    for i in range(4):
        if i % 2:
            q_copy(i).start()
        else:
            pl.when(q_mine(i))(lambda i=i: q_local(i).start())
            pl.when(jnp.logical_not(q_mine(i)))(lambda i=i: q_copy(i).start())

    for x2 in range(4):
        seg = stage[x2 * 2, 64:80, :].astype(jnp.float32)
        column = jnp.sum(
            jnp.where(lane64 == row64 + c * 64, jnp.concatenate([seg] * 4, 0), 0.0), axis=1, keepdims=True
        )
        qseg[x2] = jnp.broadcast_to(column, (PIECE, 128))
    got(kv.at[z, 1 - yl, c, CUT:PART], yb_recv)
    for d in range(2):
        pl.when(leaves(d, 0))(lambda d=d: zb(d, 0, 1 - yl).start())
    sb(0, 0, 1 - yl).start()
    pump_y(0)

    def lanes(unit):
        return [(lv, y, b) for lv, y in unit for b in range(2)]

    def scores(tile, unit):
        xt, h = tile
        q = jnp.concatenate(
            [qbuf[xt, h * HALF:(h + 1) * HALF, g * HEAD:(g + 1) * HEAD] for g in range(GROUP)], 0
        )
        keys = jnp.concatenate([kv[lv, y, b, 0:256, :] for lv, y, b in lanes(unit)], 0)
        return lax.dot_general(q, keys, (((1,), (1,)), ((), ())), preferred_element_type=jnp.float32)

    def bias(tile, unit, causal):
        xt, h = tile
        own = qseg[xt, h * HALF:(h + 1) * HALF, :]
        parts = []
        for lv, y, b in lanes(unit):
            rows = kv[lv, y, b, 256:KS, :].astype(jnp.float32)
            for half in range(2):
                same = own == rows[half:half + 1, :]
                if causal:
                    place = y * 512 + (half * 2 + lane32 // 64) * 128 + b * 64 + lane32 % 64
                    same = same & (place <= yl * 512 + xt * 128 + c * 64 + h * HALF + row32)
                parts.append(jnp.where(same, 0.0, LOW))
        return jnp.concatenate(parts, 1)

    def absorb(tile, unit, s, causal):
        at = tile[0] * 2 + tile[1]
        s = s + jnp.concatenate([bias(tile, unit, causal)] * GROUP, 0)
        before = top[at]
        now = jnp.maximum(before, jnp.max(s, axis=1, keepdims=True))
        top[at] = now
        shrink = jnp.exp2((before - now) * SLOPE)
        weights = jnp.exp2((s - now[:, :1]) * SLOPE)
        values = jnp.concatenate([kv[lv, y, b, KS:PART, :] for lv, y, b in lanes(unit)], 0)
        values = jnp.concatenate([values, jnp.ones_like(values)], 1)
        sums = jnp.dot(weights.astype(jnp.bfloat16), values, preferred_element_type=jnp.float32)
        acc[at] = acc[at] * shrink + sums[:, :HEAD]
        total[at] = total[at] * shrink + sums[:, HEAD:]

    TILED = [(xt, h) for xt in range(4) for h in range(2)]

    def compute_all(items, causal=False):
        s = scores(*items[0][:2])
        for i, (tile, unit, after) in enumerate(items):
            later = scores(*items[i + 1][:2]) if i + 1 < len(items) else None
            absorb(tile, unit, s, causal)
            if after is not None:
                after()
            s = later

    def compute(unit, tiles=TILED, causal=False):
        compute_all([(tile, unit, None) for tile in tiles], causal)

    def both(k):
        return used(0, k) & used(1, k)

    def unit_a(k):
        return [(level(0, k), yl), (level(1, k), yl)]

    def unit_b(k):
        two = both(k)
        return [
            (level(0, k), jnp.where(two, 1 - yl, yl)),
            (jnp.where(two, level(1, k), level(0, k)), 1 - yl),
        ]

    pump_a(1)
    await_a(0)
    await_b(0)
    got(qbuf, q_recv)
    compute([(z, 0), (z, 1)], causal=True)
    pump_b(1)

    def step(k, carry):
        pump_a(k)
        await_a(k - 1)
        pl.when(both(k - 1))(lambda: compute(unit_a(k - 1)))
        pump_b(k)
        pump_y(k - 1)

        @pl.when(k >= 3)
        def _():
            await_b(k - 2)
            pl.when(used(0, k - 2))(lambda: compute(unit_b(k - 2)))
        return carry

    lax.fori_loop(2, 5, step, 0)

    r, home = x % 2, x // 2

    def block(i):
        return (x + (2, 1, 3, 0)[i]) % 4

    def o_copy(i, h):
        dst = out_ref.at[
            pl.ds(pl.multiple_of(c * PIECE + h * HALF, HALF), HALF),
            pl.ds(pl.multiple_of(r * WIDE, WIDE), WIDE),
        ]
        xt = block(i)
        return (
            outbuf.at[xt, h * HALF:(h + 1) * HALF], dst, o_send, o_recv,
            dev(z, yl, xt, yh, home),
        )

    def l_copy(i):
        xt = block(i)
        return lsend.at[xt], lrecv.at[r * 2 + c], l_send, l_recv, dev(z, yl, xt, yh, home)

    def leave(i, copy):
        if i < 3:
            remote(*copy).start()
        else:
            src, dst, _, rsem, _ = copy
            pl.when(home == c)(lambda: pltpu.make_async_copy(src, dst, rsem).start())
            pl.when(home != c)(lambda: remote(*copy).start())

    def finish(i, h):
        xt = block(i)
        lines = jnp.zeros((16, 128), jnp.float32) if h == 0 else lsend[xt]
        sums = total[xt * 2 + h]
        done = (acc[xt * 2 + h] * (1.0 / sums)).astype(jnp.bfloat16)
        logs = top[xt * 2 + h] * FACTOR + jnp.log(sums)
        for g in range(GROUP):
            rows = slice(g * HALF, (g + 1) * HALF)
            outbuf[xt, h * HALF:(h + 1) * HALF, g * HEAD:(g + 1) * HEAD] = done[rows, :]
            line = jnp.sum(
                jnp.where(lane32 == row32 + c * 64 + h * HALF, logs[rows, :], 0.0), axis=0, keepdims=True
            )
            lines = lines + jnp.where(row16 == r * GROUP + g, line, 0.0)
        lsend[xt] = lines
        leave(i, o_copy(i, h))
        if h == 1:
            leave(i, l_copy(i))

    pump_y(4)
    await_b(3)
    pl.when(used(0, 3))(lambda: compute(unit_b(3)))

    @pl.when(used(0, 4))
    def _():
        await_a(4)
        await_b(4)
        unit = [(level(0, 4), 0), (level(0, 4), 1)]
        compute_all([
            ((block(i), h), unit, lambda i=i, h=h: finish(i, h)) for i in range(4) for h in range(2)
        ])

    @pl.when(jnp.logical_not(used(0, 4)))
    def _():
        for i in range(4):
            for h in range(2):
                finish(i, h)

    pl.when(s1_mine)(lambda: got(stage.at[0:7], s1_send))
    pl.when(jnp.logical_not(s1_mine))(lambda: got(stage, s1_send))
    pl.when(home == c)(lambda: got(qbuf.at[0:3], q_send))
    pl.when(home != c)(lambda: got(qbuf, q_send))

    @pl.when(used(0, 4))
    def _():
        yc(0, 4).wait_send()
        sa(0, 4).wait_send()
        got_two(sb_send.at[0])
        sc(0, 4).wait_send()

    y_rest().wait_send()

    @pl.when(home == c)
    def _():
        got(outbuf.at[0:3], o_send)
        got(lsend.at[0:3], l_send)

    @pl.when(home != c)
    def _():
        got(outbuf, o_send)
        got(lsend, l_send)

    got(lrecv, l_recv)
    lse_ref[...] = (lrecv[0] + lrecv[1] + lrecv[2] + lrecv[3])[:2 * GROUP, :]
    got(outbuf, o_recv)


def shards(queries, keys_values, segment_ids):
    pieces = jnp.transpose(keys_values, (2, 1, 0, 3)).reshape(KV_HEADS, 64, HEAD)
    marks = jnp.broadcast_to(segment_ids.astype(jnp.bfloat16)[None, None, :], (KV_HEADS, 16, 128))
    kvp = jnp.concatenate([pieces, marks], axis=1)
    dma = pltpu.SemaphoreType.DMA
    bf, f32 = jnp.bfloat16, jnp.float32
    return pl.pallas_call(
        kernel,
        out_shape=(
            jax.ShapeDtypeStruct((128, 2 * WIDE), bf),
            jax.ShapeDtypeStruct((2 * GROUP, 128), f32),
        ),
        in_specs=[pl.BlockSpec(memory_space=pl.ANY)] * 2,
        out_specs=(pl.BlockSpec(memory_space=pl.ANY), pl.BlockSpec(memory_space=pltpu.VMEM)),
        scratch_shapes=[
            pltpu.VMEM((4, PIECE, WIDE), bf),
            pltpu.VMEM((8, 80, 128), bf),
            pltpu.VMEM((Z, YL, CORES, PART, HEAD), bf),
            pltpu.VMEM((4, PIECE, 128), f32),
            pltpu.VMEM((TILES, ROWS, HEAD), f32),
            pltpu.VMEM((TILES, ROWS, 128), f32),
            pltpu.VMEM((TILES, ROWS, 128), f32),
            pltpu.VMEM((4, PIECE, WIDE), bf),
            pltpu.VMEM((4, 16, 128), f32),
            pltpu.VMEM((4, 16, 128), f32),
            dma, dma, dma, dma, dma, dma, dma, dma,
        ] + [dma((2,)), dma((2, 4))] * 2 + [dma((2,)), dma((2, 5)), dma, dma] + [dma((2,)), dma((2, 5))] * 3,
        compiler_params=pltpu.CompilerParams(
            collective_id=0, has_side_effects=True, vmem_limit_bytes=48 * 2**20
        ),
        cost_estimate=pl.CostEstimate(flops=6 * 10**9, bytes_accessed=10**6, transcendentals=12 * 10**6),
    )(queries, kvp)


def solution(mesh):
    placed = (P("ctx", "tp"), P(("ctx", "tp"), None, None, None), P("ctx"))
    return jax.shard_map(
        shards,
        mesh=mesh,
        in_specs=placed,
        out_specs=(P("ctx", "tp"), P("tp", "ctx")),
        check_vma=False,
    )
```

```python
import jax
import jax.numpy as jnp
from jax import lax
from jax.experimental import pallas as pl
from jax.experimental.pallas import tpu as pltpu
from jax.sharding import PartitionSpec as P

Q_HEADS = 48
KV_HEADS = 8
HEAD = 128
GROUP = Q_HEADS // KV_HEADS
WIDE = GROUP * HEAD
Z, YL, X, YH, CORES = 8, 2, 4, 2, 2
PIECE = 64
HALF = 32
ROWS = GROUP * HALF
TILES = 8
KS = 272
PART = 528
CUT = 352
FACTOR = HEAD ** (-0.5)
SLOPE = FACTOR * 1.4426950408889634
LOW = -1e30
MESH = pl.DeviceIdType.MESH


def kernel(
    q_ref, pieces, out_ref, lse_ref,
    qbuf, stage, kv, qseg, acc, top, total, outbuf, lsend, lrecv,
    s1_send, s1_recv, q_send, q_recv, o_send, o_recv, l_send, l_recv,
    za_send, za_recv, zb_send, zb_recv, y_send, y_recv, yb_send, yb_recv,
    sa_send, sa_recv, sb_send, sb_recv, sc_send, sc_recv,
):
    ctx = lax.axis_index("ctx")
    tp = lax.axis_index("tp")
    z, yl, x = ctx // 8, (ctx // 4) % 2, ctx % 4
    yh, c = tp // 2, tp % 2

    def dev(z_, yl_, x_, yh_, c_):
        return (z_ * 8 + yl_ * 4 + x_, yh_ * 2 + c_)

    z_up, z_down = (z + 1) % 8, (z + 7) % 8
    up_dev = dev(z_up, yl, x, yh, c)
    down_dev = dev(z_down, yl, x, yh, c)
    y_dev = dev(z, 1 - yl, x, yh, c)
    core_dev = dev(z, yl, x, yh, 1 - c)

    barrier = pltpu.get_barrier_semaphore()
    for dx in range(4):
        for dt in range(4):
            if dx or dt:
                to = (z * 8 + yl * 4 + (x + dx) % 4, (tp + dt) % 4)
                pl.semaphore_signal(barrier, inc=1, device_id=to, device_id_type=MESH)
    for to in (up_dev, down_dev, y_dev):
        pl.semaphore_signal(barrier, inc=1, device_id=to, device_id_type=MESH)

    acc[...] = jnp.zeros_like(acc)
    total[...] = jnp.zeros_like(total)
    top[...] = jnp.full_like(top, LOW)
    pl.semaphore_wait(barrier, 18)

    def remote(src, dst, ssem, rsem, to):
        return pltpu.make_async_remote_copy(
            src_ref=src, dst_ref=dst, send_sem=ssem, recv_sem=rsem, device_id=to, device_id_type=MESH
        )

    def s1_copy(i):
        x2, yh2 = (x + i % 4) % 4, (yh + i // 4) % 2
        return remote(
            pieces.at[yh2 * 4 + x2], stage.at[x * 2 + c], s1_send, s1_recv,
            dev(z, yl, x2, yh2, yh),
        )

    def s1_local():
        return pltpu.make_async_copy(pieces.at[yh * 4 + x], stage.at[x * 2 + c], s1_recv)

    def q_parts(i):
        r, c2 = i // 2, (c + i % 2) % 2
        src = q_ref.at[
            pl.ds(pl.multiple_of(c2 * PIECE, PIECE), PIECE), r * WIDE:(r + 1) * WIDE
        ]
        return src, 2 * c + r, c2

    def q_copy(i):
        src, x2, c2 = q_parts(i)
        return remote(src, qbuf.at[x], q_send, q_recv, dev(z, yl, x2, yh, c2))

    def q_local(i):
        return pltpu.make_async_copy(q_parts(i)[0], qbuf.at[x], q_recv)

    def q_mine(i):
        return (2 * c + i // 2 == x) if i % 2 == 0 else (c != c)

    s1_mine = c == yh
    pl.when(s1_mine)(lambda: s1_local().start())
    pl.when(jnp.logical_not(s1_mine))(lambda: s1_copy(0).start())
    for i in range(1, 8):
        s1_copy(i).start()
    lane16 = lax.broadcasted_iota(jnp.int32, (16, 128), 1)
    row16 = lax.broadcasted_iota(jnp.int32, (16, 128), 0)
    lane64 = lax.broadcasted_iota(jnp.int32, (PIECE, 128), 1)
    row64 = lax.broadcasted_iota(jnp.int32, (PIECE, 128), 0)
    lane32 = lax.broadcasted_iota(jnp.int32, (HALF, 128), 1)
    row32 = lax.broadcasted_iota(jnp.int32, (HALF, 128), 0)

    pltpu.make_async_copy(stage, stage, s1_recv).wait()
    mine = kv.at[z, yl, c]
    segs = []
    for x2 in range(4):
        for c2 in range(2):
            at = x2 * 64 + c2 * 32
            mine[at:at + 32, :] = stage[x2 * 2 + c2, 0:32, :]
            mine[KS + at:KS + at + 32, :] = stage[x2 * 2 + c2, 32:64, :]
        seg = stage[x2 * 2, 64:80, :].astype(jnp.float32)
        segs.append(jnp.where(c == x2 % 2, seg, pltpu.roll(seg, 64, axis=1)))
    first = jnp.where(lane16 < 64, segs[0], segs[1])
    second = jnp.where(lane16 < 64, segs[2], segs[3])
    mine[256:KS, :] = jnp.where(row16 == 0, first, second).astype(jnp.bfloat16)

    def level(d, k):
        return z - k if d == 0 else (z + k) % 8

    def arrives(d, k):
        if d == 0:
            return z - k >= 0
        return (level(1, k) <= 2) & (k <= 3) & (k >= 1)

    def used(d, k):
        if d == 0:
            return z - k >= 0
        return arrives(1, k) & (level(1, k) < z)

    def leaves(d, k):
        if d == 0:
            return (z - k >= 0) & (z < 7) & (k <= 3)
        return (level(1, k) <= 2) & (k <= 2)

    def za(d, k):
        ref = kv.at[level(d, k), yl, c, 0:CUT]
        return remote(ref, ref, za_send.at[d], za_recv.at[d, k], (up_dev, down_dev)[d])

    def zb(d, k, y):
        ref = kv.at[level(d, k), y, c, CUT:PART]
        return remote(ref, ref, zb_send.at[d], zb_recv.at[d, k], (up_dev, down_dev)[d])

    def yc(d, k):
        ref = kv.at[level(d, k), yl, c, 0:CUT]
        return remote(ref, ref, y_send.at[d], y_recv.at[d, k], y_dev)

    def y_rest():
        ref = kv.at[z, yl, c, CUT:PART]
        return remote(ref, ref, yb_send, yb_recv, y_dev)

    def sa(d, k):
        ref = kv.at[level(d, k), yl, c, 0:CUT]
        return remote(ref, ref, sa_send.at[d], sa_recv.at[d, k], core_dev)

    def sb(d, k, y):
        ref = kv.at[level(d, k), y, c, CUT:PART]
        return remote(ref, ref, sb_send.at[d], sb_recv.at[d, k], core_dev)

    def sc(d, k):
        ref = kv.at[level(d, k), 1 - yl, c, 0:CUT]
        return remote(ref, ref, sc_send.at[d], sc_recv.at[d, k], core_dev)

    def got(ref, sem):
        pltpu.make_async_copy(ref, ref, sem).wait()

    def got_two(sem):
        got(kv.at[0, 0, 0, 0:2 * (PART - CUT)], sem)

    def pump_a(k):
        for d in range(2):
            @pl.when(leaves(d, k - 1))
            def _():
                za(d, k - 1).wait_send()

            @pl.when(arrives(d, k))
            def _():
                got(kv.at[level(d, k), yl, c, 0:CUT], za_recv.at[d, k - 1])
                pl.when(leaves(d, k))(lambda: za(d, k).start())

            @pl.when(used(d, k - 1))
            def _():
                yc(d, k - 1).wait_send()
                sa(d, k - 1).wait_send()

            @pl.when(used(d, k))
            def _():
                yc(d, k).start()
                sa(d, k).start()

    def pump_b(k):
        for d in range(2):
            @pl.when(leaves(d, k - 1))
            def _():
                got_two(zb_send.at[d])

            @pl.when(arrives(d, k))
            def _():
                got_two(zb_recv.at[d, k - 1])

                @pl.when(leaves(d, k))
                def _():
                    zb(d, k, yl).start()
                    zb(d, k, 1 - yl).start()

            pl.when(used(d, k - 1))(lambda: got_two(sb_send.at[d]))

            @pl.when(used(d, k))
            def _():
                sb(d, k, yl).start()
                sb(d, k, 1 - yl).start()

    def pump_y(k):
        for d in range(2):
            pl.when(used(d, k - 1) & (k >= 1))(lambda: sc(d, k - 1).wait_send())

            @pl.when(used(d, k))
            def _():
                got(kv.at[level(d, k), 1 - yl, c, 0:CUT], y_recv.at[d, k])
                sc(d, k).start()

    def await_a(k):
        for d in range(2):
            @pl.when(used(d, k))
            def _():
                got(kv.at[level(d, k), yl, 1 - c, 0:CUT], sa_recv.at[d, k])
                got_two(sb_recv.at[d, k])

    def await_b(k):
        for d in range(2):
            @pl.when(used(d, k))
            def _():
                got(kv.at[level(d, k), 1 - yl, 1 - c, 0:CUT], sc_recv.at[d, k])

    for d in range(2):
        pl.when(leaves(d, 0))(lambda d=d: za(d, 0).start())
    y_rest().start()
    for d in range(2):
        pl.when(leaves(d, 0))(lambda d=d: zb(d, 0, yl).start())
    yc(0, 0).start()
    sa(0, 0).start()
    sb(0, 0, yl).start()
    for i in range(4):
        if i % 2:
            q_copy(i).start()
        else:
            pl.when(q_mine(i))(lambda i=i: q_local(i).start())
            pl.when(jnp.logical_not(q_mine(i)))(lambda i=i: q_copy(i).start())

    for x2 in range(4):
        seg = stage[x2 * 2, 64:80, :].astype(jnp.float32)
        column = jnp.sum(
            jnp.where(lane64 == row64 + c * 64, jnp.concatenate([seg] * 4, 0), 0.0), axis=1, keepdims=True
        )
        qseg[x2] = jnp.broadcast_to(column, (PIECE, 128))
    got(kv.at[z, 1 - yl, c, CUT:PART], yb_recv)
    for d in range(2):
        pl.when(leaves(d, 0))(lambda d=d: zb(d, 0, 1 - yl).start())
    sb(0, 0, 1 - yl).start()
    pump_y(0)

    def lanes(unit):
        return [(lv, y, b) for lv, y in unit for b in range(2)]

    def scores(tile, unit):
        xt, h = tile
        q = jnp.concatenate(
            [qbuf[xt, h * HALF:(h + 1) * HALF, g * HEAD:(g + 1) * HEAD] for g in range(GROUP)], 0
        )
        keys = jnp.concatenate([kv[lv, y, b, 0:256, :] for lv, y, b in lanes(unit)], 0)
        return lax.dot_general(q, keys, (((1,), (1,)), ((), ())), preferred_element_type=jnp.float32)

    def bias(tile, unit, causal):
        xt, h = tile
        own = qseg[xt, h * HALF:(h + 1) * HALF, :]
        parts = []
        for lv, y, b in lanes(unit):
            rows = kv[lv, y, b, 256:KS, :].astype(jnp.float32)
            for half in range(2):
                same = own == rows[half:half + 1, :]
                if causal:
                    place = y * 512 + (half * 2 + lane32 // 64) * 128 + b * 64 + lane32 % 64
                    same = same & (place <= yl * 512 + xt * 128 + c * 64 + h * HALF + row32)
                parts.append(jnp.where(same, 0.0, LOW))
        return jnp.concatenate(parts, 1)

    def absorb(tile, unit, s, causal):
        at = tile[0] * 2 + tile[1]
        s = s + jnp.concatenate([bias(tile, unit, causal)] * GROUP, 0)
        before = top[at]
        now = jnp.maximum(before, jnp.max(s, axis=1, keepdims=True))
        top[at] = now
        shrink = jnp.exp2((before - now) * SLOPE)
        weights = jnp.exp2((s - now[:, :1]) * SLOPE)
        values = jnp.concatenate([kv[lv, y, b, KS:PART, :] for lv, y, b in lanes(unit)], 0)
        values = jnp.concatenate([values, jnp.ones_like(values)], 1)
        sums = jnp.dot(weights.astype(jnp.bfloat16), values, preferred_element_type=jnp.float32)
        acc[at] = acc[at] * shrink + sums[:, :HEAD]
        total[at] = total[at] * shrink + sums[:, HEAD:]

    TILED = [(xt, h) for xt in range(4) for h in range(2)]

    def compute_all(items, causal=False):
        s = scores(*items[0][:2])
        for i, (tile, unit, after) in enumerate(items):
            later = scores(*items[i + 1][:2]) if i + 1 < len(items) else None
            absorb(tile, unit, s, causal)
            if after is not None:
                after()
            s = later

    def compute(unit, tiles=TILED, causal=False):
        compute_all([(tile, unit, None) for tile in tiles], causal)

    def both(k):
        return used(0, k) & used(1, k)

    def unit_a(k):
        return [(level(0, k), yl), (level(1, k), yl)]

    def unit_b(k):
        two = both(k)
        return [
            (level(0, k), jnp.where(two, 1 - yl, yl)),
            (jnp.where(two, level(1, k), level(0, k)), 1 - yl),
        ]

    pump_a(1)
    await_a(0)
    await_b(0)
    got(qbuf, q_recv)
    pump_b(1)
    compute([(z, 0), (z, 1)], causal=True)

    def step(k, carry):
        pump_a(k)
        pump_y(k - 1)
        await_a(k - 1)
        pl.when(both(k - 1))(lambda: compute(unit_a(k - 1)))
        pump_b(k)
        pl.when(k == 4)(lambda: pump_y(4))
        done = k - 1

        @pl.when((done >= 1) & used(0, done))
        def _():
            await_b(done)
            compute(unit_b(done))

        return carry

    lax.fori_loop(2, 5, step, 0)

    r, home = x % 2, x // 2

    def block(i):
        return (x + (2, 1, 3, 0)[i]) % 4

    def o_copy(i, h):
        dst = out_ref.at[
            pl.ds(pl.multiple_of(c * PIECE + h * HALF, HALF), HALF),
            pl.ds(pl.multiple_of(r * WIDE, WIDE), WIDE),
        ]
        xt = block(i)
        return (
            outbuf.at[xt, h * HALF:(h + 1) * HALF], dst, o_send, o_recv,
            dev(z, yl, xt, yh, home),
        )

    def l_copy(i):
        xt = block(i)
        return lsend.at[xt], lrecv.at[r * 2 + c], l_send, l_recv, dev(z, yl, xt, yh, home)

    def leave(i, copy):
        if i < 3:
            remote(*copy).start()
        else:
            src, dst, _, rsem, _ = copy
            pl.when(home == c)(lambda: pltpu.make_async_copy(src, dst, rsem).start())
            pl.when(home != c)(lambda: remote(*copy).start())

    def finish(i, h):
        xt = block(i)
        lines = jnp.zeros((16, 128), jnp.float32) if h == 0 else lsend[xt]
        sums = total[xt * 2 + h]
        done = (acc[xt * 2 + h] * (1.0 / sums)).astype(jnp.bfloat16)
        logs = top[xt * 2 + h] * FACTOR + jnp.log(sums)
        for g in range(GROUP):
            rows = slice(g * HALF, (g + 1) * HALF)
            outbuf[xt, h * HALF:(h + 1) * HALF, g * HEAD:(g + 1) * HEAD] = done[rows, :]
            line = jnp.sum(
                jnp.where(lane32 == row32 + c * 64 + h * HALF, logs[rows, :], 0.0), axis=0, keepdims=True
            )
            lines = lines + jnp.where(row16 == r * GROUP + g, line, 0.0)
        lsend[xt] = lines
        leave(i, o_copy(i, h))
        if h == 1:
            leave(i, l_copy(i))


    @pl.when(used(0, 4))
    def _():
        await_a(4)
        await_b(4)
        unit = [(level(0, 4), 0), (level(0, 4), 1)]
        compute_all([
            ((block(i), h), unit, lambda i=i, h=h: finish(i, h)) for i in range(4) for h in range(2)
        ])

    @pl.when(jnp.logical_not(used(0, 4)))
    def _():
        for i in range(4):
            for h in range(2):
                finish(i, h)

    pl.when(s1_mine)(lambda: got(stage.at[0:7], s1_send))
    pl.when(jnp.logical_not(s1_mine))(lambda: got(stage, s1_send))
    pl.when(home == c)(lambda: got(qbuf.at[0:3], q_send))
    pl.when(home != c)(lambda: got(qbuf, q_send))

    @pl.when(used(0, 4))
    def _():
        yc(0, 4).wait_send()
        sa(0, 4).wait_send()
        got_two(sb_send.at[0])
        sc(0, 4).wait_send()

    y_rest().wait_send()

    @pl.when(home == c)
    def _():
        got(outbuf.at[0:3], o_send)
        got(lsend.at[0:3], l_send)

    @pl.when(home != c)
    def _():
        got(outbuf, o_send)
        got(lsend, l_send)

    got(lrecv, l_recv)
    lse_ref[...] = (lrecv[0] + lrecv[1] + lrecv[2] + lrecv[3])[:2 * GROUP, :]
    got(outbuf, o_recv)


def shards(queries, keys_values, segment_ids):
    pieces = jnp.transpose(keys_values, (2, 1, 0, 3)).reshape(KV_HEADS, 64, HEAD)
    marks = jnp.broadcast_to(segment_ids.astype(jnp.bfloat16)[None, None, :], (KV_HEADS, 16, 128))
    kvp = jnp.concatenate([pieces, marks], axis=1)
    dma = pltpu.SemaphoreType.DMA
    bf, f32 = jnp.bfloat16, jnp.float32
    return pl.pallas_call(
        kernel,
        out_shape=(
            jax.ShapeDtypeStruct((128, 2 * WIDE), bf),
            jax.ShapeDtypeStruct((2 * GROUP, 128), f32),
        ),
        in_specs=[pl.BlockSpec(memory_space=pl.ANY)] * 2,
        out_specs=(pl.BlockSpec(memory_space=pl.ANY), pl.BlockSpec(memory_space=pltpu.VMEM)),
        scratch_shapes=[
            pltpu.VMEM((4, PIECE, WIDE), bf),
            pltpu.VMEM((8, 80, 128), bf),
            pltpu.VMEM((Z, YL, CORES, PART, HEAD), bf),
            pltpu.VMEM((4, PIECE, 128), f32),
            pltpu.VMEM((TILES, ROWS, HEAD), f32),
            pltpu.VMEM((TILES, ROWS, 128), f32),
            pltpu.VMEM((TILES, ROWS, 128), f32),
            pltpu.VMEM((4, PIECE, WIDE), bf),
            pltpu.VMEM((4, 16, 128), f32),
            pltpu.VMEM((4, 16, 128), f32),
            dma, dma, dma, dma, dma, dma, dma, dma,
        ] + [dma((2,)), dma((2, 4))] * 2 + [dma((2,)), dma((2, 5)), dma, dma] + [dma((2,)), dma((2, 5))] * 3,
        compiler_params=pltpu.CompilerParams(
            collective_id=0, has_side_effects=True, vmem_limit_bytes=48 * 2**20
        ),
        cost_estimate=pl.CostEstimate(flops=6 * 10**9, bytes_accessed=10**6, transcendentals=12 * 10**6),
    )(queries, kvp)


def solution(mesh):
    placed = (P("ctx", "tp"), P(("ctx", "tp"), None, None, None), P("ctx"))
    return jax.shard_map(
        shards,
        mesh=mesh,
        in_specs=placed,
        out_specs=(P("ctx", "tp"), P("tp", "ctx")),
        check_vma=False,
    )
```

```python
import jax
import jax.numpy as jnp
from jax import lax
from jax.experimental import pallas as pl
from jax.experimental.pallas import tpu as pltpu
from jax.sharding import PartitionSpec as P

Q_HEADS = 48
KV_HEADS = 8
HEAD = 128
GROUP = Q_HEADS // KV_HEADS
WIDE = GROUP * HEAD
Z, YL, X, YH, CORES = 8, 2, 4, 2, 2
PIECE = 64
HALF = 32
ROWS = GROUP * HALF
TILES = 8
KS = 272
PART = 528
CUT = 352
FACTOR = HEAD ** (-0.5)
SLOPE = FACTOR * 1.4426950408889634
LOW = -1e30
MESH = pl.DeviceIdType.MESH


def kernel(
    q_ref, pieces, out_ref, lse_ref,
    qbuf, stage, kv, qseg, acc, top, total, outbuf, lsend, lrecv,
    s1_send, s1_recv, q_send, q_recv, o_send, o_recv, l_send, l_recv,
    za_send, za_recv, zb_send, zb_recv, y_send, y_recv, yb_send, yb_recv,
    sa_send, sa_recv, sb_send, sb_recv, sc_send, sc_recv,
):
    ctx = lax.axis_index("ctx")
    tp = lax.axis_index("tp")
    z, yl, x = ctx // 8, (ctx // 4) % 2, ctx % 4
    yh, c = tp // 2, tp % 2

    def dev(z_, yl_, x_, yh_, c_):
        return (z_ * 8 + yl_ * 4 + x_, yh_ * 2 + c_)

    z_up, z_down = (z + 1) % 8, (z + 7) % 8
    up_dev = dev(z_up, yl, x, yh, c)
    down_dev = dev(z_down, yl, x, yh, c)
    y_dev = dev(z, 1 - yl, x, yh, c)
    core_dev = dev(z, yl, x, yh, 1 - c)

    barrier = pltpu.get_barrier_semaphore()
    for dx in range(4):
        for dt in range(4):
            if dx or dt:
                to = (z * 8 + yl * 4 + (x + dx) % 4, (tp + dt) % 4)
                pl.semaphore_signal(barrier, inc=1, device_id=to, device_id_type=MESH)
    for to in (up_dev, down_dev, y_dev):
        pl.semaphore_signal(barrier, inc=1, device_id=to, device_id_type=MESH)

    acc[...] = jnp.zeros_like(acc)
    total[...] = jnp.zeros_like(total)
    top[...] = jnp.full_like(top, LOW)
    pl.semaphore_wait(barrier, 18)

    def remote(src, dst, ssem, rsem, to):
        return pltpu.make_async_remote_copy(
            src_ref=src, dst_ref=dst, send_sem=ssem, recv_sem=rsem, device_id=to, device_id_type=MESH
        )

    def s1_copy(i):
        x2, yh2 = (x + i % 4) % 4, (yh + i // 4) % 2
        return remote(
            pieces.at[yh2 * 4 + x2], stage.at[x * 2 + c], s1_send, s1_recv,
            dev(z, yl, x2, yh2, yh),
        )

    def s1_local():
        return pltpu.make_async_copy(pieces.at[yh * 4 + x], stage.at[x * 2 + c], s1_recv)

    def q_parts(i):
        r, c2 = i // 2, (c + i % 2) % 2
        src = q_ref.at[
            pl.ds(pl.multiple_of(c2 * PIECE, PIECE), PIECE), r * WIDE:(r + 1) * WIDE
        ]
        return src, 2 * c + r, c2

    def q_copy(i):
        src, x2, c2 = q_parts(i)
        return remote(src, qbuf.at[x], q_send, q_recv, dev(z, yl, x2, yh, c2))

    def q_local(i):
        return pltpu.make_async_copy(q_parts(i)[0], qbuf.at[x], q_recv)

    def q_mine(i):
        return (2 * c + i // 2 == x) if i % 2 == 0 else (c != c)

    s1_mine = c == yh
    pl.when(s1_mine)(lambda: s1_local().start())
    pl.when(jnp.logical_not(s1_mine))(lambda: s1_copy(0).start())
    for i in range(1, 8):
        s1_copy(i).start()
    lane16 = lax.broadcasted_iota(jnp.int32, (16, 128), 1)
    row16 = lax.broadcasted_iota(jnp.int32, (16, 128), 0)
    lane64 = lax.broadcasted_iota(jnp.int32, (PIECE, 128), 1)
    row64 = lax.broadcasted_iota(jnp.int32, (PIECE, 128), 0)
    lane32 = lax.broadcasted_iota(jnp.int32, (HALF, 128), 1)
    row32 = lax.broadcasted_iota(jnp.int32, (HALF, 128), 0)

    pltpu.make_async_copy(stage, stage, s1_recv).wait()
    mine = kv.at[z, yl, c]
    segs = []
    for x2 in range(4):
        for c2 in range(2):
            at = x2 * 64 + c2 * 32
            mine[at:at + 32, :] = stage[x2 * 2 + c2, 0:32, :]
            mine[KS + at:KS + at + 32, :] = stage[x2 * 2 + c2, 32:64, :]
        seg = stage[x2 * 2, 64:80, :].astype(jnp.float32)
        segs.append(jnp.where(c == x2 % 2, seg, pltpu.roll(seg, 64, axis=1)))
    first = jnp.where(lane16 < 64, segs[0], segs[1])
    second = jnp.where(lane16 < 64, segs[2], segs[3])
    mine[256:KS, :] = jnp.where(row16 == 0, first, second).astype(jnp.bfloat16)

    def level(d, k):
        return z - k if d == 0 else (z + k) % 8

    def arrives(d, k):
        if d == 0:
            return z - k >= 0
        return (level(1, k) <= 2) & (k <= 3) & (k >= 1)

    def used(d, k):
        if d == 0:
            return z - k >= 0
        return arrives(1, k) & (level(1, k) < z)

    def leaves(d, k):
        if d == 0:
            return (z - k >= 0) & (z < 7) & (k <= 3)
        return (level(1, k) <= 2) & (k <= 2)

    def za(d, k):
        ref = kv.at[level(d, k), yl, c, 0:CUT]
        return remote(ref, ref, za_send.at[d], za_recv.at[d, k], (up_dev, down_dev)[d])

    def zb(d, k, y):
        ref = kv.at[level(d, k), y, c, CUT:PART]
        return remote(ref, ref, zb_send.at[d], zb_recv.at[d, k], (up_dev, down_dev)[d])

    def yc(d, k):
        ref = kv.at[level(d, k), yl, c, 0:CUT]
        return remote(ref, ref, y_send.at[d], y_recv.at[d, k], y_dev)

    def y_rest():
        ref = kv.at[z, yl, c, CUT:PART]
        return remote(ref, ref, yb_send, yb_recv, y_dev)

    def sa(d, k):
        ref = kv.at[level(d, k), yl, c, 0:CUT]
        return remote(ref, ref, sa_send.at[d], sa_recv.at[d, k], core_dev)

    def sb(d, k, y):
        ref = kv.at[level(d, k), y, c, CUT:PART]
        return remote(ref, ref, sb_send.at[d], sb_recv.at[d, k], core_dev)

    def sc(d, k):
        ref = kv.at[level(d, k), 1 - yl, c, 0:CUT]
        return remote(ref, ref, sc_send.at[d], sc_recv.at[d, k], core_dev)

    def got(ref, sem):
        pltpu.make_async_copy(ref, ref, sem).wait()

    def got_two(sem):
        got(kv.at[0, 0, 0, 0:2 * (PART - CUT)], sem)

    def pump_a(k):
        for d in range(2):
            @pl.when(leaves(d, k - 1))
            def _():
                za(d, k - 1).wait_send()

            @pl.when(arrives(d, k))
            def _():
                got(kv.at[level(d, k), yl, c, 0:CUT], za_recv.at[d, k - 1])
                pl.when(leaves(d, k))(lambda: za(d, k).start())

            @pl.when(used(d, k - 1))
            def _():
                yc(d, k - 1).wait_send()
                sa(d, k - 1).wait_send()

            @pl.when(used(d, k))
            def _():
                yc(d, k).start()
                sa(d, k).start()

    def pump_b(k):
        for d in range(2):
            @pl.when(leaves(d, k - 1))
            def _():
                got_two(zb_send.at[d])

            @pl.when(arrives(d, k))
            def _():
                got_two(zb_recv.at[d, k - 1])

                @pl.when(leaves(d, k))
                def _():
                    zb(d, k, yl).start()
                    zb(d, k, 1 - yl).start()

            pl.when(used(d, k - 1))(lambda: got_two(sb_send.at[d]))

            @pl.when(used(d, k))
            def _():
                sb(d, k, yl).start()
                sb(d, k, 1 - yl).start()

    def pump_y(k):
        for d in range(2):
            pl.when(used(d, k - 1) & (k >= 1))(lambda: sc(d, k - 1).wait_send())

            @pl.when(used(d, k))
            def _():
                got(kv.at[level(d, k), 1 - yl, c, 0:CUT], y_recv.at[d, k])
                sc(d, k).start()

    def await_a(k):
        for d in range(2):
            @pl.when(used(d, k))
            def _():
                got(kv.at[level(d, k), yl, 1 - c, 0:CUT], sa_recv.at[d, k])
                got_two(sb_recv.at[d, k])

    def await_b(k):
        for d in range(2):
            @pl.when(used(d, k))
            def _():
                got(kv.at[level(d, k), 1 - yl, 1 - c, 0:CUT], sc_recv.at[d, k])

    for d in range(2):
        pl.when(leaves(d, 0))(lambda d=d: za(d, 0).start())
    y_rest().start()
    for d in range(2):
        pl.when(leaves(d, 0))(lambda d=d: zb(d, 0, yl).start())
    yc(0, 0).start()
    sa(0, 0).start()
    sb(0, 0, yl).start()
    for i in range(4):
        if i % 2:
            q_copy(i).start()
        else:
            pl.when(q_mine(i))(lambda i=i: q_local(i).start())
            pl.when(jnp.logical_not(q_mine(i)))(lambda i=i: q_copy(i).start())

    for x2 in range(4):
        seg = stage[x2 * 2, 64:80, :].astype(jnp.float32)
        column = jnp.sum(
            jnp.where(lane64 == row64 + c * 64, jnp.concatenate([seg] * 4, 0), 0.0), axis=1, keepdims=True
        )
        qseg[x2] = jnp.broadcast_to(column, (PIECE, 128))
    got(kv.at[z, 1 - yl, c, CUT:PART], yb_recv)
    for d in range(2):
        pl.when(leaves(d, 0))(lambda d=d: zb(d, 0, 1 - yl).start())
    sb(0, 0, 1 - yl).start()
    pump_y(0)

    def lanes(unit):
        return [(lv, y, b) for lv, y in unit for b in range(2)]

    def scores(tile, unit):
        xt, h = tile
        q = jnp.concatenate(
            [qbuf[xt, h * HALF:(h + 1) * HALF, g * HEAD:(g + 1) * HEAD] for g in range(GROUP)], 0
        )
        keys = jnp.concatenate([kv[lv, y, b, 0:256, :] for lv, y, b in lanes(unit)], 0)
        return lax.dot_general(q, keys, (((1,), (1,)), ((), ())), preferred_element_type=jnp.float32)

    def documents(unit):
        rows = [kv[lv, y, b, 256:KS, :].astype(jnp.float32) for lv, y, b in lanes(unit)]
        return [row[half:half + 1, :] for row in rows for half in range(2)]

    def mask(s, tile, unit, causal):
        xt, h = tile
        own = qseg[xt, h * HALF:(h + 1) * HALF, :]
        marks = documents(unit)
        if not causal:
            own = jnp.concatenate([own] * GROUP, 0)
            same = jnp.concatenate([own] * len(marks), 1) == jnp.concatenate(marks, 1)
            return jnp.where(same, s, LOW)
        parts = []
        for i, mark in enumerate(marks):
            y, b, half = unit[i // 4][1], i // 2 % 2, i % 2
            place = y * 512 + (half * 2 + lane32 // 64) * 128 + b * 64 + lane32 % 64
            near = place <= yl * 512 + xt * 128 + c * 64 + h * HALF + row32
            parts.append(jnp.where((own == mark) & near, 0.0, LOW))
        return s + jnp.concatenate([jnp.concatenate(parts, 1)] * GROUP, 0)

    def absorb(tile, unit, s, causal):
        at = tile[0] * 2 + tile[1]
        s = mask(s, tile, unit, causal)
        before = top[at]
        now = jnp.maximum(before, jnp.max(s, axis=1, keepdims=True))
        top[at] = now
        shrink = jnp.exp2((before - now) * SLOPE)
        weights = jnp.exp2((s - jnp.concatenate([now] * 8, 1)) * SLOPE)
        values = jnp.concatenate([kv[lv, y, b, KS:PART, :] for lv, y, b in lanes(unit)], 0)
        values = jnp.concatenate([values, jnp.ones_like(values)], 1)
        sums = jnp.dot(weights.astype(jnp.bfloat16), values, preferred_element_type=jnp.float32)
        acc[at] = acc[at] * shrink + sums[:, :HEAD]
        total[at] = total[at] * shrink + sums[:, HEAD:]

    TILED = [(xt, h) for xt in range(4) for h in range(2)]

    def compute_all(items, causal=False):
        s = scores(*items[0][:2])
        for i, (tile, unit, after) in enumerate(items):
            later = scores(*items[i + 1][:2]) if i + 1 < len(items) else None
            absorb(tile, unit, s, causal)
            if after is not None:
                after()
            s = later

    def compute(unit, tiles=TILED, causal=False):
        compute_all([(tile, unit, None) for tile in tiles], causal)

    def both(k):
        return used(0, k) & used(1, k)

    def unit_a(k):
        return [(level(0, k), yl), (level(1, k), yl)]

    def unit_b(k):
        two = both(k)
        return [
            (level(0, k), jnp.where(two, 1 - yl, yl)),
            (jnp.where(two, level(1, k), level(0, k)), 1 - yl),
        ]

    pump_a(1)
    await_a(0)
    await_b(0)
    got(qbuf, q_recv)
    pump_b(1)
    compute([(z, 0), (z, 1)], causal=True)

    def step(k, carry):
        pump_a(k)
        pump_y(k - 1)
        await_a(k - 1)
        pl.when(both(k - 1))(lambda: compute(unit_a(k - 1)))
        pump_b(k)
        pl.when(k == 4)(lambda: pump_y(4))
        done = k - 1

        @pl.when((done >= 1) & used(0, done))
        def _():
            await_b(done)
            compute(unit_b(done))

        return carry

    lax.fori_loop(2, 5, step, 0)

    r, home = x % 2, x // 2

    def block(i):
        return (x + (2, 1, 3, 0)[i]) % 4

    def o_copy(i, h):
        dst = out_ref.at[
            pl.ds(pl.multiple_of(c * PIECE + h * HALF, HALF), HALF),
            pl.ds(pl.multiple_of(r * WIDE, WIDE), WIDE),
        ]
        xt = block(i)
        return (
            outbuf.at[xt, h * HALF:(h + 1) * HALF], dst, o_send, o_recv,
            dev(z, yl, xt, yh, home),
        )

    def l_copy(i):
        xt = block(i)
        return lsend.at[xt], lrecv.at[r * 2 + c], l_send, l_recv, dev(z, yl, xt, yh, home)

    def leave(i, copy):
        if i < 3:
            remote(*copy).start()
        else:
            src, dst, _, rsem, _ = copy
            pl.when(home == c)(lambda: pltpu.make_async_copy(src, dst, rsem).start())
            pl.when(home != c)(lambda: remote(*copy).start())

    def finish(i, h):
        xt = block(i)
        lines = jnp.zeros((16, 128), jnp.float32) if h == 0 else lsend[xt]
        sums = total[xt * 2 + h]
        done = (acc[xt * 2 + h] * (1.0 / sums)).astype(jnp.bfloat16)
        logs = top[xt * 2 + h] * FACTOR + jnp.log(sums)
        for g in range(GROUP):
            rows = slice(g * HALF, (g + 1) * HALF)
            outbuf[xt, h * HALF:(h + 1) * HALF, g * HEAD:(g + 1) * HEAD] = done[rows, :]
            line = jnp.sum(
                jnp.where(lane32 == row32 + c * 64 + h * HALF, logs[rows, :], 0.0), axis=0, keepdims=True
            )
            lines = lines + jnp.where(row16 == r * GROUP + g, line, 0.0)
        lsend[xt] = lines
        leave(i, o_copy(i, h))
        if h == 1:
            leave(i, l_copy(i))


    @pl.when(used(0, 4))
    def _():
        await_a(4)
        await_b(4)
        unit = [(level(0, 4), 0), (level(0, 4), 1)]
        compute_all([
            ((block(i), h), unit, lambda i=i, h=h: finish(i, h)) for i in range(4) for h in range(2)
        ])

    @pl.when(jnp.logical_not(used(0, 4)))
    def _():
        for i in range(4):
            for h in range(2):
                finish(i, h)

    pl.when(s1_mine)(lambda: got(stage.at[0:7], s1_send))
    pl.when(jnp.logical_not(s1_mine))(lambda: got(stage, s1_send))
    pl.when(home == c)(lambda: got(qbuf.at[0:3], q_send))
    pl.when(home != c)(lambda: got(qbuf, q_send))

    @pl.when(used(0, 4))
    def _():
        yc(0, 4).wait_send()
        sa(0, 4).wait_send()
        got_two(sb_send.at[0])
        sc(0, 4).wait_send()

    y_rest().wait_send()

    @pl.when(home == c)
    def _():
        got(outbuf.at[0:3], o_send)
        got(lsend.at[0:3], l_send)

    @pl.when(home != c)
    def _():
        got(outbuf, o_send)
        got(lsend, l_send)

    got(lrecv, l_recv)
    lse_ref[...] = (lrecv[0] + lrecv[1] + lrecv[2] + lrecv[3])[:2 * GROUP, :]
    got(outbuf, o_recv)


def shards(queries, keys_values, segment_ids):
    pieces = jnp.transpose(keys_values, (2, 1, 0, 3)).reshape(KV_HEADS, 64, HEAD)
    marks = jnp.broadcast_to(segment_ids.astype(jnp.bfloat16)[None, None, :], (KV_HEADS, 16, 128))
    kvp = jnp.concatenate([pieces, marks], axis=1)
    dma = pltpu.SemaphoreType.DMA
    bf, f32 = jnp.bfloat16, jnp.float32
    return pl.pallas_call(
        kernel,
        out_shape=(
            jax.ShapeDtypeStruct((128, 2 * WIDE), bf),
            jax.ShapeDtypeStruct((2 * GROUP, 128), f32),
        ),
        in_specs=[pl.BlockSpec(memory_space=pl.ANY)] * 2,
        out_specs=(pl.BlockSpec(memory_space=pl.ANY), pl.BlockSpec(memory_space=pltpu.VMEM)),
        scratch_shapes=[
            pltpu.VMEM((4, PIECE, WIDE), bf),
            pltpu.VMEM((8, 80, 128), bf),
            pltpu.VMEM((Z, YL, CORES, PART, HEAD), bf),
            pltpu.VMEM((4, PIECE, 128), f32),
            pltpu.VMEM((TILES, ROWS, HEAD), f32),
            pltpu.VMEM((TILES, ROWS, 128), f32),
            pltpu.VMEM((TILES, ROWS, 128), f32),
            pltpu.VMEM((4, PIECE, WIDE), bf),
            pltpu.VMEM((4, 16, 128), f32),
            pltpu.VMEM((4, 16, 128), f32),
            dma, dma, dma, dma, dma, dma, dma, dma,
        ] + [dma((2,)), dma((2, 4))] * 2 + [dma((2,)), dma((2, 5)), dma, dma] + [dma((2,)), dma((2, 5))] * 3,
        compiler_params=pltpu.CompilerParams(
            collective_id=0, has_side_effects=True, vmem_limit_bytes=48 * 2**20
        ),
        cost_estimate=pl.CostEstimate(flops=6 * 10**9, bytes_accessed=10**6, transcendentals=12 * 10**6),
    )(queries, kvp)


def solution(mesh):
    placed = (P("ctx", "tp"), P(("ctx", "tp"), None, None, None), P("ctx"))
    return jax.shard_map(
        shards,
        mesh=mesh,
        in_specs=placed,
        out_specs=(P("ctx", "tp"), P("tp", "ctx")),
        check_vma=False,
    )
```
